128 devices in a mesh: pair: 2 (over core), side: 2 (over y_lo), tp: 32 (over z, y_hi, x).
Axes of the slice: x: 4, y: 4 (y_hi: 2, y_lo: 2; y = y_hi * 2 + y_lo), z: 4, core: 2. Of those that a mesh axis runs over, the one named last changes fastest.
Arguments:
- tokens: bfloat16 [16, 256, 8192], P(('pair', 'side')), may hold values from -6 to 6
- norm_gain: float32 [8192], replicated, may hold values from 0.5 to 1.5
- w_qkv: bfloat16 [8192, 10240], P(('pair', 'side', 'tp')), may hold values from -0.25 to 0.25
- qkv_bias: bfloat16 [10240], replicated, may hold values from -8 to 8
- w_out: bfloat16 [8192, 8192], P(('pair', 'side'), 'tp'), may hold values from -0.125 to 0.125
Outputs:
- block_out: bfloat16 [16, 256, 8192], P(('pair', 'side'), None, 'tp')
The draws below stay inside these ranges and needn't reach their ends.
All inputs are finite; a program needn't handle non-finite values.
Results may differ from the reference program's by a relative error of at most 0.023.
Values may be sent and summed in bfloat16 or wider, within the bound.
No kernel may reach another device: no remote copies, remote signals or barrier semaphores. Data moves between devices by JAX's collectives and lax.ppermute only.
A program may use at most 192 MiB of HBM per device.

```python
import jax
import jax.numpy as jnp
from jax import lax

D = 8192
HEADS = 64
KV_HEADS = 8
HD = 128
SPAN = 256
SEQS = 16
N_TP = 32


def draw_qkv_bias(key, part):
    key = jax.random.fold_in(key, 7)
    base_key, sign_key, pick_key, kamp_key, qamp_key = jax.random.split(key, 5)
    q_width = HEADS * HD
    kv_width = KV_HEADS * HD
    group_size = HEADS // KV_HEADS
    base_draw = jnp.clip(0.5 * jax.random.normal(base_key, (q_width + 2 * kv_width,), jnp.float32), -3.0, 3.0)
    lowest, highest = (3.0, 5.5)
    sign_table = (2 * jax.random.randint(sign_key, (KV_HEADS, HD), 0, 2) - 1).astype(jnp.float32)
    pair_index = jnp.arange(HD, dtype=jnp.int32) % (HD // 2)
    slow_dims = pair_index >= HD // 4
    ranking = jax.random.permutation(pick_key, KV_HEADS)
    chosen = ranking < KV_HEADS // 2
    key_amp = jax.random.uniform(kamp_key, (KV_HEADS,), jnp.float32, lowest, highest)
    query_amp = jax.random.uniform(qamp_key, (HEADS,), jnp.float32, lowest, highest)
    key_mask = chosen[:, None] & slow_dims[None, :]
    key_bias = jnp.where(key_mask, key_amp[:, None] * sign_table, base_draw[q_width:q_width + kv_width].reshape(KV_HEADS, HD))
    query_mask = jnp.repeat(chosen, group_size)[:, None] & slow_dims[None, :]
    query_signs = jnp.repeat(sign_table, group_size, axis=0)
    query_bias = jnp.where(query_mask, query_amp[:, None] * query_signs, base_draw[:q_width].reshape(HEADS, HD))
    return jnp.concatenate([query_bias.reshape(-1), key_bias.reshape(-1), base_draw[q_width + kv_width:]]).astype(jnp.bfloat16)


def raised(values, key, source, target, shards_of, factor):
    owner, partner = [(jnp.arange(values.shape[axis_at]) // (values.shape[axis_at] // shards_of)).reshape([-1 if axis == axis_at else 1 for axis in range(values.ndim)]) for axis_at in (source, target)]
    chosen = jax.random.permutation(key, shards_of)[partner]
    strong = (owner == chosen) | (owner == (partner + shards_of // 2) % shards_of)
    return jnp.where(strong, factor * values, values)


def level_of(stream_key, shape, cuts, low, top_value):
    factor_of = 1.0
    for dim, parts in cuts:
        heights = jax.random.uniform(jax.random.fold_in(jax.random.fold_in(stream_key, 6), dim), (parts,), jnp.float32, low / len(cuts), top_value / len(cuts))
        factor_of = factor_of * jnp.repeat(jnp.exp(heights), shape[dim] // parts).reshape((-1,) + (1,) * (len(shape) - 1 - dim))
    return factor_of


def centred(own_key, shape, spread, limit, cuts=(), kind=jnp.bfloat16):
    drawn = spread * jax.random.normal(own_key, shape, jnp.float32)
    if cuts:
        drawn = drawn * level_of(own_key, shape, cuts, -0.22, 0.18)
    return jnp.clip(drawn, -limit, limit).astype(kind)


def gaussian_with(stream_key, shape, deviation, most, cuts, heavy, kind=jnp.bfloat16):
    drawn = deviation * jax.random.normal(stream_key, shape, jnp.float32)
    if cuts:
        drawn = drawn * level_of(stream_key, shape, cuts, -0.22, 0.18)
    return jnp.clip(raised(drawn, jax.random.fold_in(stream_key, 3), *heavy), -most, most).astype(kind)


def setup_inputs(seed: int = 0) -> dict:
    key_list = jax.random.split(jax.random.key(seed), 6)
    tokens = centred(key_list[0], (SEQS, SPAN, D), 1.0, 6.0, ((0, 4),))
    norm_gain = jnp.clip(1.0 + 0.1 * jax.random.normal(key_list[1], (D,), jnp.float32), 0.5, 1.5)
    w_qkv = gaussian_with(key_list[2], (D, HEADS * HD + 2 * KV_HEADS * HD), D ** -0.5, 0.25, ((0, 128),), (0, 1, 128, 5.5))
    qkv_bias = draw_qkv_bias(jax.random.fold_in(key_list[5], 71), 0)
    w_out = gaussian_with(key_list[4], (HEADS * HD, D), (HEADS * HD) ** -0.5, 0.125, ((0, 4), (1, 32)), (0, 1, 32, 2.75))
    return {"tokens": tokens, "norm_gain": norm_gain, "w_qkv": w_qkv, "qkv_bias": qkv_bias, "w_out": w_out}


def rotate_pairs(values, positions):
    half_size = values.shape[-1] // 2
    inverse = 1000000.0 ** (-jnp.arange(half_size, dtype=jnp.float32) * 2.0 / values.shape[-1])
    angles = positions.astype(jnp.float32)[:, None] * inverse[None, :]
    cosine = jnp.cos(angles)[None, :, None, :]
    sine = jnp.sin(angles)[None, :, None, :]
    first_half = values[..., :half_size]
    second_half = values[..., half_size:]
    return jnp.concatenate([first_half * cosine - second_half * sine, second_half * cosine + first_half * sine], -1)

def reference(tokens, norm_gain, w_qkv, qkv_bias, w_out):
    seq_count, span_len, width = tokens.shape
    q_width = HEADS * HD
    kv_width = KV_HEADS * HD
    inputs = tokens.astype(jnp.float32)
    mean_square = lax.optimization_barrier(jnp.mean(inputs * inputs, axis=-1, keepdims=True))
    normed = (inputs * lax.rsqrt(mean_square + 1e-06) * norm_gain).astype(jnp.bfloat16)
    flat_rows = normed.reshape(seq_count * span_len, width)
    projected = jnp.dot(flat_rows, w_qkv, preferred_element_type=jnp.float32) + qkv_bias.astype(jnp.float32)
    positions = jnp.arange(span_len)
    query = rotate_pairs(projected[:, :q_width].reshape(seq_count, span_len, HEADS, HD), positions).astype(jnp.bfloat16)
    keys = rotate_pairs(projected[:, q_width:q_width + kv_width].reshape(seq_count, span_len, KV_HEADS, HD), positions).astype(jnp.bfloat16)
    values_bf = projected[:, q_width + kv_width:].reshape(seq_count, span_len, KV_HEADS, HD).astype(jnp.bfloat16)
    group_size = HEADS // KV_HEADS
    keys_all = jnp.repeat(keys, group_size, axis=2).astype(jnp.float32)
    values_all = jnp.repeat(values_bf, group_size, axis=2).astype(jnp.float32)
    scores = jnp.einsum('sqhd,skhd->shqk', query.astype(jnp.float32), keys_all) * HD ** (-0.5)
    causal = jnp.arange(span_len)[:, None] >= jnp.arange(span_len)[None, :]
    scores = jnp.where(causal[None, None], scores, -1e+30)
    scores = scores - lax.optimization_barrier(jnp.max(scores, axis=-1, keepdims=True))
    expo = jnp.exp(scores)
    weights = (expo / lax.optimization_barrier(jnp.sum(expo, axis=-1, keepdims=True))).astype(jnp.bfloat16)
    attended = jnp.einsum('shqk,skhd->sqhd', weights.astype(jnp.float32), values_all).astype(jnp.bfloat16)
    attended = attended.reshape(seq_count * span_len, q_width)
    slice_width = q_width // N_TP

    def add_group(group_idx, running):
        cols_part = lax.dynamic_slice_in_dim(attended, group_idx * slice_width, slice_width, 1)
        rows_part = lax.dynamic_slice_in_dim(w_out, group_idx * slice_width, slice_width, 0)
        partial_term = jnp.dot(cols_part, rows_part, preferred_element_type=jnp.float32).astype(jnp.bfloat16)
        partial_term = lax.optimization_barrier(partial_term)
        return running + partial_term.astype(jnp.float32)
    summed = lax.fori_loop(0, N_TP, add_group, jnp.zeros((seq_count * span_len, width), jnp.float32))
    return (inputs + summed.reshape(seq_count, span_len, width)).astype(jnp.bfloat16)
```

```python
import functools

import jax
import jax.numpy as jnp
import numpy as np
from jax import lax
from jax.experimental import pallas as pl
from jax.experimental.pallas import tpu as pltpu
from jax.sharding import PartitionSpec as P

HD = 128
SPAN = 256
D = 8192
BF = jnp.bfloat16
F32 = jnp.float32
VMEM_LIMIT = 56 * 1024 * 1024


def rope_tables():
    half = HD // 2
    inverse = 1000000.0 ** (-np.arange(half, dtype=np.float64) * 2.0 / HD)
    angles = (
        np.arange(SPAN, dtype=np.float32)[:, None] * inverse.astype(np.float32)[None, :]
    )
    angles = angles.astype(np.float64)
    return np.cos(angles).astype(np.float32), np.sin(angles).astype(np.float32)


def kv_lanes(part):
    low = list(range(16 * part, 16 * part + 16))
    return low + [64 + i for i in low] + list(range(128 + 32 * part, 160 + 32 * part))


def tables():
    cosine, sine = rope_tables()
    pack = np.zeros((2, 256, 512), np.float32)
    gather = np.zeros((4, 2, 128, 256), np.float32)
    bias_sel = np.zeros((4, 256, 128), np.float32)
    k_cos = np.ones((4, SPAN, 128), np.float32)
    k_sin = np.zeros((4, SPAN, 128), np.float32)
    turn = np.zeros((64, 64), np.float32)
    for lane in range(16):
        turn[lane + 16, lane] = 1.0
        turn[lane, lane + 16] = 1.0
    for part in range(4):
        lanes = kv_lanes(part)
        for lane, column in enumerate(lanes):
            pack[0, column, part * 128 + lane] = 1.0
            pack[1, column, part * 128 + 64 + lane] = 1.0
            gather[part, 0, lane, column] = 1.0
            gather[part, 1, 64 + lane, column] = 1.0
            bias_sel[part, column, lane] = 1.0
        bias_sel[part, :, 64:] = bias_sel[part, :, :64] @ turn
        dims = slice(16 * part, 16 * part + 16)
        for base in (0, 64):
            k_cos[part, :, base : base + 16] = cosine[:, dims]
            k_cos[part, :, base + 16 : base + 32] = cosine[:, dims]
            k_sin[part, :, base : base + 16] = -sine[:, dims]
            k_sin[part, :, base + 16 : base + 32] = sine[:, dims]
    unpack = np.zeros((128, 256), np.float32)
    unpack[:64, :64] = np.eye(64)
    unpack[:64, 64:128] = turn
    unpack[64:, 128:192] = np.eye(64)
    unpack[64:, 192:] = turn
    q_cos = np.concatenate([cosine, cosine], 1)
    q_sin = np.concatenate([-sine, sine], 1)
    return {
        "pack": jnp.asarray(pack, BF),
        "gather": jnp.asarray(gather, BF),
        "bias_sel": jnp.asarray(bias_sel, BF),
        "unpack": jnp.asarray(unpack, BF),
        "k_cos": jnp.asarray(k_cos),
        "k_sin": jnp.asarray(k_sin),
        "q_cos": jnp.asarray(q_cos),
        "q_sin": jnp.asarray(q_sin),
    }


def dot(a, b):
    return jnp.dot(a, b, preferred_element_type=F32)


def params(**kw):
    return pltpu.CompilerParams(vmem_limit_bytes=VMEM_LIMIT, **kw)


def full(shape):
    return pl.BlockSpec(shape, lambda *_: (0,) * len(shape))


def pack_body(wq, wk, wv, gain, sel, kv, q0, q1):
    scale = gain[...]
    for i in range(4):
        for h, out in enumerate((q0, q1)):
            lanes = slice((2 * i + h) * 128, (2 * i + h + 1) * 128)
            out[i] = (wq[:, lanes].astype(F32) * scale).astype(BF)
    both = jnp.concatenate([wk[...], wv[...]], 1).astype(F32) * scale
    both = both.astype(BF)
    packed = dot(both[:32], sel[0]) + dot(both[32:], sel[1])
    for i in range(4):
        kv[i] = packed[:, i * 128 : (i + 1) * 128].astype(BF)


def pack(w_qkv, gain, sel):
    return pl.pallas_call(
        pack_body,
        grid=(8,),
        in_specs=[
            pl.BlockSpec((64, 1024), lambda g: (0, g)),
            pl.BlockSpec((64, 128), lambda g: (0, 64 + g)),
            pl.BlockSpec((64, 128), lambda g: (0, 72 + g)),
            full((64, 1)),
            full((2, 256, 512)),
        ],
        out_specs=[
            pl.BlockSpec((4, 32, 128), lambda g: (g, 0, 0)),
            pl.BlockSpec((4, 64, 128), lambda g: (g, 0, 0)),
            pl.BlockSpec((4, 64, 128), lambda g: (g, 0, 0)),
        ],
        out_shape=[
            jax.ShapeDtypeStruct((32, 32, 128), BF),
            jax.ShapeDtypeStruct((32, 64, 128), BF),
            jax.ShapeDtypeStruct((32, 64, 128), BF),
        ],
        compiler_params=params(),
        name="pack_weights",
        cost_estimate=pl.CostEstimate(flops=1 << 26, bytes_accessed=3 << 20, transcendentals=0),
    )(w_qkv, w_qkv, w_qkv, gain, sel)


def kv_body(idx, xa, xb, w0, w1, w2, w3, unpack, bk, bv, bsel, cos, sin, kv, norm_a, norm_b, ws):
    @pl.when(pl.program_id(0) == 0)
    def _():
        for j, w in enumerate((w0, w1, w2, w3)):
            both = dot(w[...], unpack[...]).astype(BF)
            ws[j, :, :32, :] = both[:, :128].reshape(32, 32, 128)
            ws[j, :, 32:, :] = both[:, 128:].reshape(32, 32, 128)

    bias = jnp.concatenate([bk[0], bv[0]], 1)
    bias = dot(jnp.broadcast_to(bias, (16, 256)), bsel[0])[0:1]
    lane = lax.broadcasted_iota(jnp.int32, (128, 128), 1)
    cosine = cos[0]
    sine = sin[0]
    parts = []
    for x, norm in ((xa, norm_a), (xb, norm_b)):
        square = jnp.zeros((128, 128), F32)
        for c in range(64):
            piece = x[:, c * 128 : (c + 1) * 128].astype(F32)
            square += piece * piece
        mean = jnp.sum(square, axis=1, keepdims=True) * (1.0 / D)
        inv = lax.rsqrt(mean + 1e-6)
        norm[...] = jnp.broadcast_to(inv, (128, 128))
        acc = jnp.zeros((128, 128), F32)
        for j in range(4):
            start = pl.multiple_of(idx[j] * 2048, 2048)
            acc += dot(x[:, pl.ds(start, 2048)], ws[j].reshape(2048, 128))
        parts.append(acc * inv + bias)
    a, b = parts
    left = a * cosine + pltpu.roll(a, 64, 1) * sine
    right = pltpu.roll(b, 64, 1) * cosine + b * sine
    kv[...] = jnp.where(lane < 64, left, right).astype(BF)


def keys_values(idx, x, ws, tab, bias):
    return pl.pallas_call(
        kv_body,
        grid_spec=pltpu.PrefetchScalarGridSpec(
            num_scalar_prefetch=1,
            grid=(4,),
            in_specs=[
                pl.BlockSpec((128, D), lambda i, idx: (i, 0)),
                pl.BlockSpec((128, D), lambda i, idx: (i + 4, 0)),
                *[full((1024, 128))] * 4,
                full((128, 256)),
                pl.BlockSpec((1, 1, 128), lambda i, idx: (64 + idx[5], 0, 0)),
                pl.BlockSpec((1, 1, 128), lambda i, idx: (72 + idx[5], 0, 0)),
                pl.BlockSpec((1, 256, 128), lambda i, idx: (idx[6], 0, 0)),
                pl.BlockSpec((1, 128, 128), lambda i, idx: (idx[6], i % 2, 0)),
                pl.BlockSpec((1, 128, 128), lambda i, idx: (idx[6], i % 2, 0)),
            ],
            out_specs=[
                pl.BlockSpec((128, 128), lambda i, idx: (i, 0)),
                pl.BlockSpec((128, 128), lambda i, idx: (i, 0)),
                pl.BlockSpec((128, 128), lambda i, idx: (i, 0)),
            ],
            scratch_shapes=[pltpu.VMEM((4, 32, 64, 128), BF)],
        ),
        out_shape=[
            jax.ShapeDtypeStruct((512, 128), BF),
            jax.ShapeDtypeStruct((512, 128), F32),
            jax.ShapeDtypeStruct((512, 128), F32),
        ],
        compiler_params=params(),
        name="keys_values",
        cost_estimate=pl.CostEstimate(
            flops=2 * 1024 * 8192 * 256, bytes_accessed=18 << 20, transcendentals=0
        ),
    )(idx, x, x, *ws, tab["unpack"], bias, bias, tab["bias_sel"], tab["k_cos"], tab["k_sin"])


def head_body(
    idx, x, w0, w1, w2, w3, na, nb, bq, cos, sin, p0, p1, p2, p3, g0, g1, g2, g3, att
):
    seq = pl.program_id(0)
    acc = jnp.zeros((SPAN, HD), F32)
    for j, w in enumerate((w0, w1, w2, w3)):
        start = pl.multiple_of(idx[j] * 2048, 2048)
        acc += dot(x[:, pl.ds(start, 2048)], w[...])
    norm = jnp.where(seq < 2, na[...], nb[...])
    query = acc * norm + bq[0].astype(F32)
    query = (query * cos[...] + pltpu.roll(query, 64, 1) * sin[...]).astype(BF)
    kv = jnp.zeros((SPAN, 256), F32)
    for piece, place in ((p0, g0), (p1, g1), (p2, g2), (p3, g3)):
        kv += dot(piece[...], place[0, 0])
    keys = kv[:, :128].astype(BF)
    values = kv[:, 128:].astype(BF)
    scores = lax.dot_general(
        query, keys, (((1,), (1,)), ((), ())), preferred_element_type=F32
    ) * (HD**-0.5)
    row = lax.broadcasted_iota(jnp.int32, (SPAN, SPAN), 0)
    col = lax.broadcasted_iota(jnp.int32, (SPAN, SPAN), 1)
    scores = jnp.where(row >= col, scores, -1e30)
    scores = jnp.exp(scores - jnp.max(scores, axis=1, keepdims=True))
    weights = (scores / jnp.sum(scores, axis=1, keepdims=True)).astype(BF)
    att[...] = dot(weights, values).astype(BF)


def head(h, idx, x, ws, norms, tab, bias, pieces):
    def place(r):
        return pl.BlockSpec((1, 1, 128, 256), lambda i, idx: ((idx[6] + 4 - r) % 4, i // 2, 0, 0))

    return pl.pallas_call(
        head_body,
        grid_spec=pltpu.PrefetchScalarGridSpec(
            num_scalar_prefetch=1,
            grid=(4,),
            in_specs=[
                pl.BlockSpec((SPAN, D), lambda i, idx: (i, 0)),
                *[full((2048, 128))] * 4,
                pl.BlockSpec((SPAN, 128), lambda i, idx: (i % 2, 0)),
                pl.BlockSpec((SPAN, 128), lambda i, idx: (i % 2, 0)),
                pl.BlockSpec((1, 1, 128), lambda i, idx: (2 * idx[4] + h, 0, 0)),
                full((SPAN, 128)),
                full((SPAN, 128)),
                *[pl.BlockSpec((SPAN, 128), lambda i, idx: (i % 2, 0))] * 4,
                *[place(r) for r in range(4)],
            ],
            out_specs=pl.BlockSpec((SPAN, 128), lambda i, idx: (i, 0)),
        ),
        out_shape=jax.ShapeDtypeStruct((1024, 128), BF),
        compiler_params=params(),
        name=f"query_head_{h}",
        cost_estimate=pl.CostEstimate(
            flops=2 * 1024 * 8192 * 256, bytes_accessed=20 << 20, transcendentals=1 << 18
        ),
    )(
        idx,
        x,
        *ws,
        *norms,
        bias,
        tab["q_cos"],
        tab["q_sin"],
        *pieces,
        *[tab["gather"]] * 4,
    )


def route_body(pos, k0, r0, k1, r1, o0, o1, o2, o3, sem):
    for r, out in enumerate((o0, o1, o2, o3)):
        goal = (pos[2] + r) % 4
        same_p = goal // 2 == pos[0]
        same_s = goal % 2 == pos[1]
        for src, cond in (
            (k0, same_p & same_s),
            (r0, jnp.logical_not(same_p) & same_s),
            (k1, same_p & jnp.logical_not(same_s)),
            (r1, jnp.logical_not(same_p) & jnp.logical_not(same_s)),
        ):

            @pl.when(cond)
            def _():
                pltpu.make_async_copy(src, out, sem.at[r]).start()

    for r, out in enumerate((o0, o1, o2, o3)):
        pltpu.make_async_copy(k0, out, sem.at[r]).wait()


def route(pos, blocks):
    any_spec = pl.BlockSpec(memory_space=pl.ANY)
    return pl.pallas_call(
        route_body,
        grid_spec=pltpu.PrefetchScalarGridSpec(
            num_scalar_prefetch=1,
            grid=(),
            in_specs=[any_spec] * 4,
            out_specs=[any_spec] * 4,
            scratch_shapes=[pltpu.SemaphoreType.DMA((4,))],
        ),
        out_shape=[jax.ShapeDtypeStruct((1024, 256), BF)] * 4,
        compiler_params=params(),
        name="route_rows",
        cost_estimate=pl.CostEstimate(flops=0, bytes_accessed=4 << 20, transcendentals=0),
    )(pos, *blocks)


def out_body(idx, *refs):
    atts = refs[:8]
    own = refs[8:12]
    other = refs[12:16]
    out = refs[16]
    wv, sem = refs[17:]
    p = idx[7]

    @pl.when(pl.program_id(0) == 0)
    def _():
        copies = []
        for r in range(4):
            copies.append(
                pltpu.make_async_copy(own[r], wv.at[r, :, :, p], sem.at[r])
            )
            copies.append(
                pltpu.make_async_copy(other[r], wv.at[r, :, :, 1 - p], sem.at[4 + r])
            )
        for copy in copies:
            copy.start()
        for copy in copies:
            copy.wait()

    for r in range(4):
        acc = jnp.zeros((256, 256), F32)
        for xr in range(4):
            part = (idx[6] + 4 - xr) % 4
            for h in range(2):
                acc += dot(atts[h * 4 + xr][...], wv[r, part, h].reshape(256, 256))
        out[r] = acc.astype(BF)


def project_out(idx, atts, own, other):
    any_spec = pl.BlockSpec(memory_space=pl.ANY)
    return pl.pallas_call(
        out_body,
        grid_spec=pltpu.PrefetchScalarGridSpec(
            num_scalar_prefetch=1,
            grid=(4,),
            in_specs=[
                *[pl.BlockSpec((256, 256), lambda i, idx: (i, 0))] * 8,
                *[any_spec] * 8,
            ],
            out_specs=pl.BlockSpec((4, 256, 256), lambda i, idx: (0, i, 0)),
            scratch_shapes=[
                pltpu.VMEM((4, 4, 2, 2, 128, 256), BF),
                pltpu.SemaphoreType.DMA((8,)),
            ],
        ),
        out_shape=jax.ShapeDtypeStruct((4, 1024, 256), BF),
        compiler_params=params(),
        name="project_out",
        cost_estimate=pl.CostEstimate(
            flops=2 * 1024 * 2048 * 1024, bytes_accessed=10 << 20, transcendentals=0
        ),
    )(
        idx,
        *atts,
        *[w.reshape(4, 2, 128, 256) for w in own],
        *[w.reshape(4, 2, 128, 256) for w in other],
    )


SWAP = [(0, 1), (1, 0)]


def shift(dz, dy, dx):
    return [
        (
            z * 8 + y * 4 + x,
            (z + dz) % 4 * 8 + (y + dy) % 2 * 4 + (x + dx) % 4,
        )
        for z in range(4)
        for y in range(2)
        for x in range(4)
    ]


def shards(tokens, norm_gain, w_qkv, qkv_bias, w_out):
    tab = tables()
    seqs, span, width = tokens.shape
    p = lax.axis_index("pair")
    s = lax.axis_index("side")
    t = lax.axis_index("tp")
    z, yh, xi = t // 8, t // 4 % 2, t % 4
    idx = jnp.stack(
        [2 * p + s, 2 * (1 - p) + s, 2 * p + 1 - s, 2 * (1 - p) + 1 - s, t, t // 4, xi, p]
    ).astype(jnp.int32)
    pos = jnp.stack([p, s, z]).astype(jnp.int32)
    x = tokens.reshape(seqs * span, width)
    bias = qkv_bias.reshape(80, 1, 128)

    gain = lax.dynamic_slice_in_dim(norm_gain, (2 * p + s) * 2048 + t * 64, 64, 0)
    kv_w, q0_w, q1_w = pack(w_qkv, gain.reshape(64, 1), tab["pack"])

    def spread(w):
        rows = w.shape[0] * w.shape[1]
        own = lax.all_to_all(w, "tp", split_axis=0, concat_axis=0, tiled=True)
        own = own.reshape(rows, 128)
        side = lax.ppermute(own, "side", SWAP)
        mate = lax.ppermute(own, "pair", SWAP)
        far = lax.ppermute(side, "pair", SWAP)
        return own, mate, side, far

    kv_ws = spread(kv_w)
    q_ws = [spread(q0_w), spread(q1_w)]

    halves = w_out.reshape(2, 1024, 256)
    keep = lax.dynamic_index_in_dim(halves, p, 0, keepdims=False)
    send = lax.dynamic_index_in_dim(halves, 1 - p, 0, keepdims=False)
    recv = lax.ppermute(send, "pair", SWAP)
    keep_s = lax.ppermute(keep, "side", SWAP)
    recv_s = lax.ppermute(recv, "side", SWAP)
    routed = route(pos, (keep, recv, keep_s, recv_s))
    w_own = [routed[0]] + [
        lax.ppermute(routed[r], "tp", shift(r, 0, 0)) for r in range(1, 4)
    ]
    w_other = [lax.ppermute(w, "pair", SWAP) for w in w_own]

    kv_piece, norm_a, norm_b = keys_values(idx, x, kv_ws, tab, bias)
    pieces = [kv_piece] + [
        lax.ppermute(kv_piece, "tp", shift(0, 0, r)) for r in range(1, 4)
    ]

    atts = []
    for h in range(2):
        att = head(h, idx, x, q_ws[h], (norm_a, norm_b), tab, bias, pieces)
        across = lax.ppermute(att, "tp", shift(0, 1, 0))
        first = jnp.where(yh == 0, att, across)
        second = jnp.where(yh == 0, across, att)
        both = jnp.concatenate([first, second], 1)
        atts += [both] + [
            lax.ppermute(both, "tp", shift(0, 0, r)) for r in range(1, 4)
        ]

    partial = project_out(idx, atts, w_own, w_other)
    total = partial[0].astype(F32)
    for r in range(1, 4):
        total += lax.ppermute(partial[r], "tp", shift(-r, 0, 0)).astype(F32)
    residual = lax.dynamic_slice_in_dim(tokens, t * 256, 256, 2).astype(F32)
    return (residual + total.reshape(seqs, span, 256)).astype(BF)


def solution(mesh):
    placed = (
        P(("pair", "side"), None, None),
        P(),
        P(("pair", "side", "tp"), None),
        P(),
        P(("pair", "side"), "tp"),
    )
    return jax.shard_map(
        shards,
        mesh=mesh,
        in_specs=placed,
        out_specs=P(("pair", "side"), None, "tp"),
        check_vma=False,
    )
```

```python
import functools

import jax
import jax.numpy as jnp
import numpy as np
from jax import lax
from jax.experimental import pallas as pl
from jax.experimental.pallas import tpu as pltpu
from jax.sharding import PartitionSpec as P

HD = 128
SPAN = 256
D = 8192
BF = jnp.bfloat16
F32 = jnp.float32
VMEM_LIMIT = 22 * 1024 * 1024


def rope_tables():
    half = HD // 2
    inverse = 1000000.0 ** (-np.arange(half, dtype=np.float64) * 2.0 / HD)
    angles = (
        np.arange(SPAN, dtype=np.float32)[:, None] * inverse.astype(np.float32)[None, :]
    )
    angles = angles.astype(np.float64)
    return np.cos(angles).astype(np.float32), np.sin(angles).astype(np.float32)


def kv_lanes(part):
    low = list(range(16 * part, 16 * part + 16))
    return low + [64 + i for i in low] + list(range(128 + 32 * part, 160 + 32 * part))


def tables():
    cosine, sine = rope_tables()
    pack = np.zeros((2, 256, 512), np.float32)
    gather = np.zeros((4, 2, 128, 256), np.float32)
    bias_sel = np.zeros((4, 256, 128), np.float32)
    k_cos = np.ones((4, SPAN, 128), np.float32)
    k_sin = np.zeros((4, SPAN, 128), np.float32)
    turn = np.zeros((64, 64), np.float32)
    for lane in range(16):
        turn[lane + 16, lane] = 1.0
        turn[lane, lane + 16] = 1.0
    for part in range(4):
        lanes = kv_lanes(part)
        for lane, column in enumerate(lanes):
            pack[0, column, part * 128 + lane] = 1.0
            pack[1, column, part * 128 + 64 + lane] = 1.0
            gather[part, 0, lane, column] = 1.0
            gather[part, 1, 64 + lane, column] = 1.0
            bias_sel[part, column, lane] = 1.0
        bias_sel[part, :, 64:] = bias_sel[part, :, :64] @ turn
        dims = slice(16 * part, 16 * part + 16)
        for base in (0, 64):
            k_cos[part, :, base : base + 16] = cosine[:, dims]
            k_cos[part, :, base + 16 : base + 32] = cosine[:, dims]
            k_sin[part, :, base : base + 16] = -sine[:, dims]
            k_sin[part, :, base + 16 : base + 32] = sine[:, dims]
    unpack = np.zeros((128, 256), np.float32)
    unpack[:64, :64] = np.eye(64)
    unpack[:64, 64:128] = turn
    unpack[64:, 128:192] = np.eye(64)
    unpack[64:, 192:] = turn
    q_cos = np.concatenate([cosine, cosine], 1)
    q_sin = np.concatenate([-sine, sine], 1)
    return {
        "pack": jnp.asarray(pack, BF),
        "gather": jnp.asarray(gather, BF),
        "bias_sel": jnp.asarray(bias_sel, BF),
        "unpack": jnp.asarray(unpack, BF),
        "k_cos": jnp.asarray(k_cos),
        "k_sin": jnp.asarray(k_sin),
        "q_cos": jnp.asarray(q_cos),
        "q_sin": jnp.asarray(q_sin),
    }


def dot(a, b):
    return jnp.dot(a, b, preferred_element_type=F32)


def params(**kw):
    return pltpu.CompilerParams(vmem_limit_bytes=VMEM_LIMIT, **kw)


VM = pl.BlockSpec(memory_space=pltpu.VMEM)
SM = pl.BlockSpec(memory_space=pltpu.SMEM)
AN = pl.BlockSpec(memory_space=pl.ANY)


def shape(dims, dtype=BF):
    return jax.ShapeDtypeStruct(dims, dtype)


def cost(flops, mib, trans=0):
    return pl.CostEstimate(flops=flops, bytes_accessed=mib << 20, transcendentals=trans)


def call(body, name, in_specs, out_shape, out_specs, estimate, scratch=()):
    return pl.pallas_call(
        body,
        in_specs=in_specs,
        out_specs=out_specs,
        out_shape=out_shape,
        scratch_shapes=list(scratch),
        compiler_params=params(),
        name=name,
        cost_estimate=estimate,
    )


def pack_body(idx, w, gain, sel, after, out):
    row = gain[pl.ds(idx[0] * 16 + idx[4] // 2, 1), :]
    lane = lax.broadcasted_iota(jnp.int32, (64, 128), 1)
    sub = lax.broadcasted_iota(jnp.int32, (64, 128), 0)
    hit = lane == sub + idx[4] % 2 * 64
    scale = jnp.sum(jnp.where(hit, jnp.broadcast_to(row, (64, 128)), 0.0), axis=1, keepdims=True)
    for t in range(32):
        for h in range(2):
            lanes = slice((2 * t + h) * 128, (2 * t + h + 1) * 128)
            out[t, 32 + 64 * h : 96 + 64 * h, :] = (w[:, lanes].astype(F32) * scale).astype(BF)
    for g in range(8):
        keys = w[:, 8192 + g * 128 : 8320 + g * 128]
        values = w[:, 9216 + g * 128 : 9344 + g * 128]
        both = (jnp.concatenate([keys, values], 1).astype(F32) * scale).astype(BF)
        packed = dot(both[:32], sel[0]) + dot(both[32:], sel[1])
        for i in range(4):
            out[4 * g + i, :32, :] = packed[:, i * 128 : (i + 1) * 128].astype(BF)


def pack(idx, w_qkv, gain, sel, after):
    return call(
        pack_body,
        "pack_weights",
        [SM, VM, VM, VM, AN],
        shape((32, 160, 128)),
        VM,
        cost(1 << 26, 3),
    )(idx, w_qkv, gain, sel, after)


def cut_body(lo, hi, src, *refs):
    refs[-1][...] = src[:, lo:hi, :]


def cut(lo, hi, src, after, name):
    return call(
        functools.partial(cut_body, lo, hi),
        name,
        [VM] + [AN] * len(after),
        shape((32, hi - lo, 128)),
        VM,
        cost(0, 1),
    )(src, *after)


def norm_body(x, out):
    def step(i, _):
        rows = pl.ds(pl.multiple_of(i * 128, 128), 128)
        square = jnp.zeros((128, 128), F32)
        for c in range(64):
            piece = x[rows, c * 128 : (c + 1) * 128].astype(F32)
            square += piece * piece
        mean = jnp.sum(square, axis=1, keepdims=True) * (1.0 / D)
        out[rows, :] = jnp.broadcast_to(lax.rsqrt(mean + 1e-6), (128, 128))
        return 0

    lax.fori_loop(0, 8, step, 0)


def norms(x):
    return call(
        norm_body, "token_norms", [VM], shape((1024, 128), F32), VM, cost(1 << 25, 16)
    )(x)


def kv_body(idx, x, own, mate, side, far, norm, unpack, bias, bsel, cos, sin, kv, ws):
    acc = None
    pieces = (own[:, :32, :], mate[:, :32, :], side[...], far[...])
    for j, w in enumerate(pieces):
        both = dot(w.reshape(1024, 128), unpack[...]).astype(BF)
        ws[:, :32, :] = both[:, :128].reshape(32, 32, 128)
        ws[:, 32:, :] = both[:, 128:].reshape(32, 32, 128)
        start = pl.multiple_of(idx[j] * 2048, 2048)
        part = dot(x[:, pl.ds(start, 2048)], ws[...].reshape(2048, 128))
        acc = part if acc is None else acc + part
    g = idx[5]
    base = jnp.concatenate([bias[pl.ds(64 + g, 1), :], bias[pl.ds(72 + g, 1), :]], 1)
    base = dot(jnp.broadcast_to(base, (8, 256)).astype(BF), bsel[idx[6]])[0:1]
    cosine = cos[idx[6]]
    sine = sin[idx[6]]
    acc = acc * norm[...] + base
    lane = lax.broadcasted_iota(jnp.int32, (SPAN, 128), 1)
    for i in range(2):
        a = acc[i * 256 : (i + 1) * 256]
        b = acc[512 + i * 256 : 512 + (i + 1) * 256]
        left = a * cosine + pltpu.roll(a, 64, 1) * sine
        right = pltpu.roll(b, 64, 1) * cosine + b * sine
        kv[i * 256 : (i + 1) * 256] = jnp.where(lane < 64, left, right).astype(BF)


def keys_values(idx, x, ws, norm, tab, bias):
    return call(
        kv_body,
        "keys_values",
        [SM] + [VM] * 11,
        shape((512, 128)),
        VM,
        cost(2 * 1024 * 8192 * 256, 2),
        [pltpu.VMEM((32, 64, 128), BF)],
    )(
        idx, x, *ws, norm, tab["unpack"], bias, tab["bias_sel"], tab["k_cos"], tab["k_sin"]
    )


def join_body(idx, p0, p1, p2, p3, gather, keys, values):
    for half in range(2):
        kv = jnp.zeros((512, 256), F32)
        for r, piece in enumerate((p0, p1, p2, p3)):
            kv += dot(piece[...], gather[(idx[6] + 4 - r) % 4, half])
        keys[half * 512 : (half + 1) * 512] = kv[:, :128].astype(BF)
        values[half * 512 : (half + 1) * 512] = kv[:, 128:].astype(BF)


def join_kv(idx, pieces, tab):
    return call(
        join_body,
        "join_keys_values",
        [SM] + [VM] * 5,
        [shape((1024, 128))] * 2,
        [VM] * 2,
        cost(1 << 28, 1),
    )(idx, *pieces, tab["gather"])


def head_body(h, idx, x, own, mate, side, far, norm, bias, cos, sin, keys, values, att):
    lanes = slice(32 + 64 * h, 96 + 64 * h)
    acc = None
    for j, w in enumerate((own[:, lanes, :], mate[:, lanes, :], side[...], far[...])):
        start = pl.multiple_of(idx[j] * 2048, 2048)
        part = dot(x[:, pl.ds(start, 2048)], w.reshape(2048, 128))
        acc = part if acc is None else acc + part
    acc = acc * norm[...] + bias[pl.ds(2 * idx[4] + h, 1), :]
    row = lax.broadcasted_iota(jnp.int32, (SPAN, SPAN), 0)
    col = lax.broadcasted_iota(jnp.int32, (SPAN, SPAN), 1)
    ones = jnp.ones((SPAN, HD), BF)
    for seq in range(4):
        rows = slice(seq * SPAN, (seq + 1) * SPAN)
        query = acc[rows]
        query = (query * cos[...] + pltpu.roll(query, 64, 1) * sin[...]).astype(BF)
        scores = lax.dot_general(
            query, keys[rows], (((1,), (1,)), ((), ())), preferred_element_type=F32
        ) * (HD**-0.5)
        scores = jnp.where(row >= col, scores, -1e30)
        expo = jnp.exp(scores - jnp.max(scores, axis=1, keepdims=True)).astype(BF)
        mixed = dot(expo, jnp.concatenate([values[rows], ones], 1))
        att[rows] = (mixed[:, :HD] / mixed[:, HD:]).astype(BF)


def head(h, idx, x, ws, norm, tab, bias, keys, values):
    return call(
        functools.partial(head_body, h),
        f"query_head_{h}",
        [SM] + [VM] * 11,
        shape((1024, 128)),
        VM,
        cost(2 * 1024 * 8192 * 256, 2, 1 << 18),
    )(idx, x, *ws, norm, bias, tab["q_cos"], tab["q_sin"], keys, values)


def beside_body(idx, att, across, out):
    same = idx[8] == idx[7]
    out[:, :128] = jnp.where(same, att[...], across[...])
    out[:, 128:] = jnp.where(same, across[...], att[...])


def beside(idx, att, across, name):
    return call(
        beside_body, name, [SM, VM, VM], shape((1024, 256)), VM, cost(0, 1)
    )(idx, att, across)


def route_body(idx, keep, recv, keep_s, recv_s, *outs):
    for r, out in enumerate(outs):
        goal = (idx[9] + r) % 4
        same_pair = goal // 2 == idx[7]
        same_side = goal % 2 == idx[10]
        for ref, hit in (
            (keep, same_pair & same_side),
            (recv, jnp.logical_not(same_pair) & same_side),
            (keep_s, same_pair & jnp.logical_not(same_side)),
            (recv_s, jnp.logical_not(same_pair) & jnp.logical_not(same_side)),
        ):

            @pl.when(hit)
            def _():
                out[...] = ref[...]


def route(idx, blocks):
    return call(
        route_body,
        "route_rows",
        [SM] + [VM] * 4,
        [shape((1024, 256))] * 4,
        [VM] * 4,
        cost(0, 4),
    )(idx, *blocks)


def pick_body(idx, w, keep, send):
    p = idx[7]
    keep[...] = w[pl.ds(pl.multiple_of(p * 1024, 1024), 1024), :]
    send[...] = w[pl.ds(pl.multiple_of((1 - p) * 1024, 1024), 1024), :]


def pick(idx, w):
    return call(
        pick_body, "pick_rows", [SM, VM], [shape((1024, 256))] * 2, [VM] * 2, cost(0, 2)
    )(idx, w)


def out_body(idx, *refs):
    atts = refs[:8]
    own = refs[8:12]
    other = refs[12:16]
    outs = refs[16:]
    for r in range(4):
        acc = None
        for xr in range(4):
            part = (idx[6] + 4 - xr) % 4
            for h in range(2):
                rows = pl.ds(pl.multiple_of(part * 256 + h * 128, 128), 128)
                w = jnp.concatenate([own[r][rows, :], other[r][rows, :]], 0)
                term = dot(atts[h * 4 + xr][...], w)
                acc = term if acc is None else acc + term
        outs[r][...] = acc.astype(BF)


def project_out(idx, atts, own, other):
    return call(
        out_body,
        "project_out",
        [SM] + [VM] * 16,
        [shape((1024, 256))] * 4,
        [VM] * 4,
        cost(2 * 1024 * 2048 * 1024, 4),
    )(idx, *atts, *own, *other)


def finish_body(idx, x, p0, p1, p2, p3, out):
    total = x[:, pl.ds(pl.multiple_of(idx[4] * 256, 256), 256)].astype(F32)
    for part in (p0, p1, p2, p3):
        total += part[...].astype(F32)
    out[...] = total.astype(BF)


def finish(idx, x, parts):
    return call(
        finish_body, "add_residual", [SM] + [VM] * 5, shape((1024, 256)), VM, cost(1 << 20, 3)
    )(idx, x, *parts)


SWAP = [(0, 1), (1, 0)]


def shift(dz, dy, dx):
    return [
        (
            z * 8 + y * 4 + x,
            (z + dz) % 4 * 8 + (y + dy) % 2 * 4 + (x + dx) % 4,
        )
        for z in range(4)
        for y in range(2)
        for x in range(4)
    ]


def shards(tokens, norm_gain, w_qkv, qkv_bias, w_out):
    tab = tables()
    seqs, span, width = tokens.shape
    p = lax.axis_index("pair")
    s = lax.axis_index("side")
    t = lax.axis_index("tp")
    z, yh, xi = t // 8, t // 4 % 2, t % 4
    idx = jnp.stack(
        [
            2 * p + s,
            2 * (1 - p) + s,
            2 * p + 1 - s,
            2 * (1 - p) + 1 - s,
            t,
            t // 4,
            xi,
            p,
            yh,
            z,
            s,
        ]
    ).astype(jnp.int32)
    x = tokens.reshape(seqs * span, width)
    bias = qkv_bias.reshape(80, 128).astype(F32)

    keep, send = pick(idx, w_out)
    recv = lax.ppermute(send, "pair", SWAP)
    keep_s = lax.ppermute(keep, "side", SWAP)
    recv_s = lax.ppermute(recv, "side", SWAP)

    packed = pack(idx, w_qkv, norm_gain.reshape(64, 128), tab["pack"], recv)
    own = lax.all_to_all(packed, "tp", split_axis=0, concat_axis=0, tiled=True)
    mate = lax.ppermute(own, "pair", SWAP)
    sides, fars = [], []

    def across(lo, hi, after, name):
        side = lax.ppermute(cut(lo, hi, own, after, name), "side", SWAP)
        fars.append(lax.ppermute(side, "pair", SWAP))
        sides.append(side)

    across(0, 32, [keep_s, recv_s], "cut_kv")
    routed = route(idx, (keep, recv, keep_s, recv_s))
    across(32, 96, [sides[0]], "cut_0")
    across(96, 160, [sides[1]], "cut_1")
    w_own = [routed[0]] + [
        lax.ppermute(routed[r], "tp", shift(r, 0, 0)) for r in range(1, 4)
    ]
    w_other = [lax.ppermute(w, "pair", SWAP) for w in w_own]

    norm = norms(x)
    kv_piece = keys_values(idx, x, (own, mate, sides[0], fars[0]), norm, tab, bias)
    pieces = [kv_piece] + [
        lax.ppermute(kv_piece, "tp", shift(0, 0, r)) for r in range(1, 4)
    ]
    keys, values = join_kv(idx, pieces, tab)

    atts = []
    for h in range(2):
        ws = (own, mate, sides[1 + h], fars[1 + h])
        att = head(h, idx, x, ws, norm, tab, bias, keys, values)
        both = beside(idx, att, lax.ppermute(att, "tp", shift(0, 1, 0)), f"beside_{h}")
        atts += [both] + [
            lax.ppermute(both, "tp", shift(0, 0, r)) for r in range(1, 4)
        ]

    partial = project_out(idx, atts, w_own, w_other)
    parts = [partial[0]] + [
        lax.ppermute(partial[r], "tp", shift(-r, 0, 0)) for r in range(1, 4)
    ]
    return finish(idx, x, parts).reshape(seqs, span, 256)


def solution(mesh):
    placed = (
        P(("pair", "side"), None, None),
        P(),
        P(("pair", "side", "tp"), None),
        P(),
        P(("pair", "side"), "tp"),
    )
    return jax.shard_map(
        shards,
        mesh=mesh,
        in_specs=placed,
        out_specs=P(("pair", "side"), None, "tp"),
        check_vma=False,
    )
```

```python
import functools

import jax
import jax.numpy as jnp
import numpy as np
from jax import lax
from jax.experimental import pallas as pl
from jax.experimental.pallas import tpu as pltpu
from jax.sharding import PartitionSpec as P

HD = 128
SPAN = 256
D = 8192
BF = jnp.bfloat16
F32 = jnp.float32
TP, KV_HEAD, X, PAIR, Y_HI, Z, SIDE = range(7)
VMEM_LIMIT = 20 * 1024 * 1024


def rope_tables():
    half = HD // 2
    inverse = 1000000.0 ** (-np.arange(half, dtype=np.float64) * 2.0 / HD)
    angles = (
        np.arange(SPAN, dtype=np.float32)[:, None] * inverse.astype(np.float32)[None, :]
    )
    angles = angles.astype(np.float64)
    return np.cos(angles).astype(np.float32), np.sin(angles).astype(np.float32)


def kv_lanes(part):
    low = list(range(16 * part, 16 * part + 16))
    return low + [64 + i for i in low] + list(range(128 + 32 * part, 160 + 32 * part))


def tables():
    cosine, sine = rope_tables()
    pack = np.zeros((2, 256, 512), np.float32)
    gather = np.zeros((4, 2, 128, 256), np.float32)
    bias_sel = np.zeros((4, 256, 128), np.float32)
    k_cos = np.ones((4, SPAN, 128), np.float32)
    k_sin = np.zeros((4, SPAN, 128), np.float32)
    turn = np.zeros((64, 64), np.float32)
    for lane in range(16):
        turn[lane + 16, lane] = 1.0
        turn[lane, lane + 16] = 1.0
    for part in range(4):
        lanes = kv_lanes(part)
        for lane, column in enumerate(lanes):
            pack[0, column, part * 128 + lane] = 1.0
            pack[1, column, part * 128 + 64 + lane] = 1.0
            gather[part, 0, lane, column] = 1.0
            gather[part, 1, 64 + lane, column] = 1.0
            bias_sel[part, column, lane] = 1.0
        bias_sel[part, :, 64:] = bias_sel[part, :, :64] @ turn
        dims = slice(16 * part, 16 * part + 16)
        for base in (0, 64):
            k_cos[part, :, base : base + 16] = cosine[:, dims]
            k_cos[part, :, base + 16 : base + 32] = cosine[:, dims]
            k_sin[part, :, base : base + 16] = -sine[:, dims]
            k_sin[part, :, base + 16 : base + 32] = sine[:, dims]
    unpack = np.zeros((128, 256), np.float32)
    unpack[:64, :64] = np.eye(64)
    unpack[:64, 64:128] = turn
    unpack[64:, 128:192] = np.eye(64)
    unpack[64:, 192:] = turn
    q_cos = np.concatenate([cosine, cosine], 1)
    q_sin = np.concatenate([-sine, sine], 1)
    return {
        "pack": jnp.asarray(pack, BF),
        "gather": jnp.asarray(gather, BF),
        "bias_sel": jnp.asarray(bias_sel, BF),
        "unpack": jnp.asarray(unpack, BF),
        "k_cos": jnp.asarray(k_cos),
        "k_sin": jnp.asarray(k_sin),
        "q_cos": jnp.asarray(q_cos),
        "q_sin": jnp.asarray(q_sin),
    }


def dot(a, b):
    return jnp.dot(a, b, preferred_element_type=F32)


def params(**kw):
    return pltpu.CompilerParams(vmem_limit_bytes=VMEM_LIMIT, **kw)


VM = pl.BlockSpec(memory_space=pltpu.VMEM)
SM = pl.BlockSpec(memory_space=pltpu.SMEM)
AN = pl.BlockSpec(memory_space=pl.ANY)


def shape(dims, dtype=BF):
    return jax.ShapeDtypeStruct(dims, dtype)


def cost(mib):
    return pl.CostEstimate(flops=0, bytes_accessed=mib << 20, transcendentals=0)


def call(body, name, in_specs, out_shape, out_specs, estimate, scratch=(), after=()):
    count = len(in_specs)

    def run(*refs):
        body(*refs[:count], *refs[count + len(after) :])

    kernel = pl.pallas_call(
        run,
        in_specs=in_specs + [AN] * len(after),
        out_specs=out_specs,
        out_shape=out_shape,
        scratch_shapes=list(scratch),
        compiler_params=params(),
        name=name,
        cost_estimate=estimate,
    )
    return lambda *args: kernel(*args, *after)


def pack_body(idx, w, gain, sel, out):
    row = gain[pl.ds((2 * idx[PAIR] + idx[SIDE]) * 16 + idx[TP] // 2, 1), :]
    lane = lax.broadcasted_iota(jnp.int32, (64, 128), 1)
    sub = lax.broadcasted_iota(jnp.int32, (64, 128), 0)
    hit = lane == sub + idx[TP] % 2 * 64
    scale = jnp.sum(jnp.where(hit, jnp.broadcast_to(row, (64, 128)), 0.0), axis=1, keepdims=True)
    for t in range(32):
        place = t // 8 * 4 + t % 4
        which = pl.ds((t // 4 + idx[Y_HI]) % 2, 1)
        for h in range(2):
            lanes = slice((2 * t + h) * 128, (2 * t + h + 1) * 128)
            block = (w[:, lanes].astype(F32) * scale).astype(BF)
            out[place, which, 32 + 64 * h : 96 + 64 * h, :] = block[None]
    for g in range(8):
        keys = w[:, 8192 + g * 128 : 8320 + g * 128]
        values = w[:, 9216 + g * 128 : 9344 + g * 128]
        both = (jnp.concatenate([keys, values], 1).astype(F32) * scale).astype(BF)
        packed = dot(both[:32], sel[0]) + dot(both[32:], sel[1])
        which = pl.ds((g + idx[Y_HI]) % 2, 1)
        for i in range(4):
            block = packed[:, i * 128 : (i + 1) * 128].astype(BF)
            out[g // 2 * 4 + i, which, :32, :] = block[None]


def pack(idx, w_qkv, gain, sel):
    return call(
        pack_body,
        "pack_weights",
        [SM, VM, VM, VM],
        shape((16, 2, 160, 128)),
        VM,
        cost(0),
    )(idx, w_qkv, gain, sel)


def cut_body(src, kv, q):
    kv[...] = src[:, 1, :32, :]
    q[...] = src[:, 1, 32:, :]


def cut(src, after):
    return call(
        cut_body,
        "cut_other_half",
        [VM],
        [shape((16, 32, 128)), shape((16, 128, 128))],
        [VM] * 2,
        cost(0),
        after=after,
    )(src)


def near_body(lo, hi, src, got, out):
    out[0] = src[:, 0, lo:hi, :]
    out[1] = got[...]


def near_rows(lo, hi, src, got, after, name):
    return call(
        functools.partial(near_body, lo, hi),
        name,
        [VM, VM],
        shape((2, 16, hi - lo, 128)),
        VM,
        cost(0),
        after=after,
    )(src, got)


def row_groups(idx, own, mate, side, far):
    p, s, y = idx[PAIR], idx[SIDE], idx[Y_HI]
    for ref, core, here in ((own, p, s), (mate, 1 - p, s), (side, p, 1 - s), (far, 1 - p, 1 - s)):
        yield ref, 0, 2 * core + here, y
        yield ref, 1, 2 * core + 1 - here, 1 - y


def norm_body(idx, x, out, residual):
    def step(i, _):
        rows = pl.ds(pl.multiple_of(i * 128, 128), 128)
        square = jnp.zeros((128, 128), F32)
        for c in range(64):
            piece = x[rows, c * 128 : (c + 1) * 128].astype(F32)
            square += piece * piece
        mean = jnp.sum(square, axis=1, keepdims=True) * (1.0 / D)
        out[rows, :] = jnp.broadcast_to(lax.rsqrt(mean + 1e-6), (128, 128))
        return 0

    lax.fori_loop(0, 8, step, 0)
    residual[...] = x[:, pl.ds(pl.multiple_of(idx[TP] * 256, 256), 256)]


def norms(idx, x, after):
    return call(
        norm_body,
        "token_norms",
        [SM, VM],
        [shape((1024, 128), F32), shape((1024, 256))],
        [VM] * 2,
        cost(0),
        after=after,
    )(idx, x)


def kv_body(idx, x, own, mate, side, far, norm, unpack, bias, bsel, cos, sin, kv, ws, acc, buf, sem):
    for i in range(4):
        pltpu.make_async_copy(x.at[pl.ds(i * 128, 128)], buf.at[i], sem.at[i]).start()
    for ref, i, block, y in row_groups(idx, own, mate, side, far):
        both = dot(ref[i].reshape(512, 128), unpack[...]).astype(BF).reshape(4, 4, 32, 256)
        for z in range(4):
            ws[block, z, y, :, :32, :] = both[z, :, :, :128]
            ws[block, z, y, :, 32:, :] = both[z, :, :, 128:]
    tiles = [
        pltpu.make_async_copy(x.at[pl.ds(i * 128, 128)], buf.at[i % 4], sem.at[i])
        for i in range(8)
    ]
    for i in range(8):
        tiles[i].wait()
        sums = None
        for j in range(4):
            piece = buf[i % 4, :, j * 2048 : (j + 1) * 2048]
            part = dot(piece, ws[j].reshape(2048, 128))
            sums = part if sums is None else sums + part
        acc[i * 128 : (i + 1) * 128, :] = sums
        if i < 4:
            tiles[i + 4].start()
    g = idx[KV_HEAD]
    part = idx[X]
    base = jnp.concatenate([bias[pl.ds(64 + g, 1), :], bias[pl.ds(72 + g, 1), :]], 1)
    base = dot(jnp.broadcast_to(base, (8, 256)).astype(BF), bsel[part])[0:1]
    cosine = cos[part]
    sine = sin[part]
    acc[...] = acc[...] * norm[...] + base
    lane = lax.broadcasted_iota(jnp.int32, (SPAN, 128), 1)
    for i in range(2):
        a = acc[i * 256 : (i + 1) * 256]
        b = acc[512 + i * 256 : 512 + (i + 1) * 256]
        left = a * cosine + pltpu.roll(a, 64, 1) * sine
        right = pltpu.roll(b, 64, 1) * cosine + b * sine
        kv[i * 256 : (i + 1) * 256] = jnp.where(lane < 64, left, right).astype(BF)


def keys_values(idx, x, ws, norm, tab, bias, after):
    return call(
        kv_body,
        "keys_values",
        [SM, AN] + [VM] * 10,
        shape((512, 128)),
        VM,
        cost(0),
        [
            pltpu.VMEM((4, 4, 2, 4, 64, 128), BF),
            pltpu.VMEM((1024, 128), F32),
            pltpu.VMEM((4, 128, D), BF),
            pltpu.SemaphoreType.DMA((8,)),
        ],
        after,
    )(
        idx, x, *ws, norm, tab["unpack"], bias, tab["bias_sel"], tab["k_cos"], tab["k_sin"]
    )


def join_body(idx, kv, first, second, gather, keys, values):
    for half in range(2):
        both = jnp.zeros((512, 256), F32)
        for k, piece in enumerate((kv, first, second.at[0], second.at[1])):
            both += dot(piece[...], gather[idx[X] ^ k, half])
        keys[half * 512 : (half + 1) * 512] = both[:, :128].astype(BF)
        values[half * 512 : (half + 1) * 512] = both[:, 128:].astype(BF)


def join_kv(idx, pieces, tab, after):
    return call(
        join_body,
        "join_keys_values",
        [SM] + [VM] * 4,
        [shape((1024, 128))] * 2,
        [VM] * 2,
        cost(0),
        after=after,
    )(idx, *pieces, tab["gather"])


def heads_body(idx, x, own, mate, side, far, norm, bias, cos, sin, keys, values, *refs):
    atts, ws = refs[:2], refs[2]
    for ref, i, block, y in row_groups(idx, own, mate, side, far.at[0]):
        for z in range(4):
            for h in range(2):
                rows = ref[i, 4 * z : 4 * z + 4, 64 * h : 64 * h + 64, :]
                ws[block, z, y, :, 128 * h : 128 * h + 128] = rows.reshape(256, 128)
    acc = None
    for j in range(4):
        part = dot(x[:, j * 2048 : (j + 1) * 2048], ws[j].reshape(2048, 256))
        acc = part if acc is None else acc + part
    row = lax.broadcasted_iota(jnp.int32, (SPAN, SPAN), 0)
    col = lax.broadcasted_iota(jnp.int32, (SPAN, SPAN), 1)
    ones = jnp.ones((SPAN, HD), BF)
    for seq in range(4):
        rows = slice(seq * SPAN, (seq + 1) * SPAN)
        with_ones = jnp.concatenate([values[rows], ones], 1)
        for h, att in enumerate(atts):
            query = acc[rows, h * 128 : (h + 1) * 128] * norm[rows, :]
            query += bias[pl.ds(2 * idx[TP] + h, 1), :]
            query = (query * cos[...] + pltpu.roll(query, 64, 1) * sin[...]).astype(BF)
            scores = lax.dot_general(
                query, keys[rows], (((1,), (1,)), ((), ())), preferred_element_type=F32
            ) * (HD**-0.5)
            scores = jnp.where(row >= col, scores, -1e30)
            expo = jnp.exp(scores - jnp.max(scores, axis=1, keepdims=True)).astype(BF)
            mixed = dot(expo, with_ones)
            att[rows] = (mixed[:, :HD] / mixed[:, HD:]).astype(BF)


def heads(idx, x, ws, norm, tab, bias, keys, values, after):
    return call(
        heads_body,
        "query_heads",
        [SM] + [VM] * 11,
        [shape((1024, 128))] * 2,
        [VM] * 2,
        cost(0),
        [pltpu.VMEM((4, 4, 2, 256, 256), BF)],
        after=after,
    )(idx, x, *ws, norm, bias, tab["q_cos"], tab["q_sin"], keys, values)


def beside_body(idx, att, across, *outs):
    same = idx[Y_HI] == idx[PAIR]
    for i, out in enumerate(outs):
        rows = slice(512 * i, 512 * i + 512)
        out[:, :128] = jnp.where(same, att[rows, :], across[rows, :])
        out[:, 128:] = jnp.where(same, across[rows, :], att[rows, :])


def beside(idx, att, across, after):
    return call(
        beside_body,
        "beside",
        [SM, VM, VM],
        [shape((512, 256))] * 2,
        [VM] * 2,
        cost(0),
        after=after,
    )(idx, att, across)


def stack_body(*refs):
    for i, ref in enumerate(refs[:-1]):
        refs[-1][i] = ref[...]


def stack(name, arrays, after):
    dims = (len(arrays),) + arrays[0].shape
    return call(
        stack_body,
        name,
        [VM] * len(arrays),
        shape(dims),
        VM,
        cost(0),
        after=after,
    )(*arrays)


def gather_body(a0, a1, a2, a3, *outs):
    for i, out in enumerate(outs):
        for k, ref in enumerate((a0, a1, a2, a3)):
            out[k] = ref[512 * i : 512 * i + 512, :]


def gather_halves(arrays, after):
    return call(
        gather_body,
        "stack_head0",
        [VM] * 4,
        [shape((4, 512, 128))] * 2,
        [VM] * 2,
        cost(0),
        after=after,
    )(*arrays)


def pick_body(idx, here, across, keep, send):
    p = idx[PAIR]
    for i, w in enumerate((here, across)):
        side = idx[SIDE] if i == 0 else 1 - idx[SIDE]
        keep[side] = w[pl.ds(pl.multiple_of(p * 1024, 1024), 1024), :]
        send[side] = w[pl.ds(pl.multiple_of((1 - p) * 1024, 1024), 1024), :]


def pick(idx, here, across, after):
    return call(
        pick_body,
        "pick_rows",
        [SM, VM, VM],
        [shape((2, 1024, 256))] * 2,
        [VM] * 2,
        cost(0),
        after=after,
    )(idx, here, across)


def route_body(idx, keep, recv, *outs):
    for r, out in enumerate(outs):
        goal = (idx[Z] + r) % 4
        same = goal // 2 == idx[PAIR]

        @pl.when(same)
        def _():
            out[...] = keep[goal % 2]

        @pl.when(jnp.logical_not(same))
        def _():
            out[...] = recv[goal % 2]


def route(idx, keep, recv, after):
    return call(
        route_body,
        "route_rows",
        [SM, VM, VM],
        [shape((1024, 256))] * 4,
        [VM] * 4,
        cost(0),
        after=after,
    )(idx, keep, recv)


def w_rows(idx, own, other, r, part):
    rows = []
    for h in range(2):
        for w in (own, other):
            rows.append(w[r, pl.ds(pl.multiple_of(part * 256 + h * 128, 128), 128), :])
    return jnp.concatenate(rows, 0)


def out_body(i, idx, h0, h1, h2, h3, there, a0, a1, a2, a3, own, other, *outs):
    same = idx[Y_HI] == idx[PAIR]
    half = slice(512 * i, 512 * i + 512)
    lanes = []
    for k, (here, both) in enumerate(zip((h0, h1, h2, h3), (a0, a1, a2, a3))):
        near = here[half, :]
        far = there[k]
        lanes.append(
            jnp.concatenate(
                [jnp.where(same, near, far), jnp.where(same, far, near), both[...]], 1
            )
        )
    for r, out in enumerate(outs):
        acc = None
        for k in range(4):
            term = dot(lanes[k], w_rows(idx, own, other, r, (idx[X] + 4 - k) % 4))
            acc = term if acc is None else acc + term
        out[...] = acc.astype(BF)


def project_out(i, idx, here, there, both, own, other, after):
    return call(
        functools.partial(out_body, i),
        f"project_out_{i}",
        [SM] + [VM] * 11,
        [shape((512, 256))] * 4,
        [VM] * 4,
        cost(0),
        after=after,
    )(idx, *here, there, *both, own, other)


def finish_body(i, residual, p0, p1, p2, p3, *refs):
    total = residual[512 * i : 512 * i + 512, :].astype(F32)
    for part in (p0, p1, p2, p3):
        total += part[...].astype(F32)
    if i:
        refs[1][:512, :] = refs[0][...]
        refs[1][512:, :] = total.astype(BF)
    else:
        refs[0][...] = total.astype(BF)


def finish(i, residual, parts, former):
    return call(
        functools.partial(finish_body, i),
        f"add_residual_{i}",
        [VM] * (5 + len(former)),
        shape((512 + 512 * i, 256)),
        VM,
        cost(0),
    )(residual, *parts, *former)


SWAP = [(0, 1), (1, 0)]


def shift(dz, dy, dx):
    return [
        (
            z * 8 + y * 4 + x,
            (z + dz) % 4 * 8 + (y + dy) % 2 * 4 + (x + dx) % 4,
        )
        for z in range(4)
        for y in range(2)
        for x in range(4)
    ]


def flip(bits):
    return [(t, t ^ bits) for t in range(32)]


PLANES = [[z * 8 + y * 4 + x for z in range(4) for x in range(4)] for y in range(2)]
DIAGONAL = [
    (s * 32 + t, (1 - s) * 32 + (t ^ 4)) for s in range(2) for t in range(32)
]


def shards(tokens, norm_gain, w_qkv, qkv_bias, w_out):
    tab = tables()
    seqs, span, width = tokens.shape
    p = lax.axis_index("pair")
    s = lax.axis_index("side")
    t = lax.axis_index("tp")
    idx = jnp.stack([t, t // 4, t % 4, p, t // 4 % 2, t // 8, s]).astype(jnp.int32)
    bias = qkv_bias.reshape(80, 128).astype(F32)
    x = tokens.reshape(seqs * span, width)

    w_across = lax.ppermute(w_out, "side", SWAP)
    packed = pack(idx, w_qkv, norm_gain.reshape(64, 128), tab["pack"])
    blocks = lax.all_to_all(
        packed, "tp", split_axis=0, concat_axis=0, tiled=True, axis_index_groups=PLANES
    )
    norm, residual = norms(idx, x, [packed])
    keep, send = pick(idx, w_out, w_across, [norm])
    recv = lax.ppermute(send, "pair", SWAP)
    kv_got, q_got = [
        lax.ppermute(part, ("side", "tp"), DIAGONAL) for part in cut(blocks, [keep])
    ]
    routed = route(idx, keep, recv, [])
    kv_own = near_rows(0, 32, blocks, kv_got, [routed[0]], "near_kv")
    kv_side = lax.ppermute(kv_own, "side", SWAP)
    kv_mate = lax.ppermute(kv_own, "pair", SWAP)
    q_own = near_rows(32, 160, blocks, q_got, [kv_side], "near_q")
    q_side = lax.ppermute(q_own, "side", SWAP)
    q_mate = lax.ppermute(q_own, "pair", SWAP)
    kv_far = lax.ppermute(kv_side, "pair", SWAP)
    kv_piece = keys_values(
        idx, x, (kv_own, kv_mate, kv_side, kv_far), norm, tab, bias, [q_own]
    )
    first = lax.ppermute(kv_piece, "tp", flip(1))
    pieces = stack("stack_kv", [kv_piece, first], [])
    second = lax.ppermute(pieces, "tp", flip(2))
    keys, values = join_kv(idx, (kv_piece, first, second), tab, [])
    w_own = stack(
        "stack_rows",
        [routed[0]] + [lax.ppermute(routed[r], "tp", shift(r, 0, 0)) for r in range(1, 4)],
        [keys],
    )
    w_other = lax.ppermute(w_own, "pair", SWAP)
    q_late = stack("late_q", [q_side], [w_own])
    q_far = lax.ppermute(q_late, "pair", SWAP)
    att0, att1 = heads(
        idx, x, (q_own, q_mate, q_side, q_far), norm, tab, bias, keys, values, [q_late]
    )

    here = [att0] + [lax.ppermute(att0, "tp", shift(0, 0, r)) for r in range(1, 4)]
    stacked = gather_halves(here, [])
    there = [lax.ppermute(half, "tp", shift(0, 1, 0)) for half in stacked]
    halves = beside(idx, att1, lax.ppermute(att1, "tp", shift(0, 1, 0)), [stacked[0]])

    former = []
    done = []
    for i in range(2):
        plane = [halves[i]] + [
            lax.ppermute(halves[i], "tp", shift(0, 0, r)) for r in range(1, 4)
        ]
        partial = project_out(i, idx, here, there[i], plane, w_own, w_other, done)
        done = [partial[0]]
        parts = [partial[0]] + [
            lax.ppermute(partial[r], "tp", shift(-r, 0, 0)) for r in range(1, 4)
        ]
        former = [finish(i, residual, parts, former)]
    return former[0].reshape(seqs, span, 256)


def solution(mesh):
    placed = (
        P(("pair", "side"), None, None),
        P(),
        P(("pair", "side", "tp"), None),
        P(),
        P(("pair", "side"), "tp"),
    )
    return jax.shard_map(
        shards,
        mesh=mesh,
        in_specs=placed,
        out_specs=P(("pair", "side"), None, "tp"),
        check_vma=False,
    )
```

```python
import functools

import jax
import jax.numpy as jnp
import numpy as np
from jax import lax
from jax.experimental import pallas as pl
from jax.experimental.pallas import tpu as pltpu
from jax.sharding import PartitionSpec as P

HD = 128
SPAN = 256
D = 8192
BF = jnp.bfloat16
F32 = jnp.float32
TP, KV_HEAD, X, PAIR, Y_HI, Z, SIDE = range(7)


def rope_tables():
    half = HD // 2
    inverse = 1000000.0 ** (-np.arange(half, dtype=np.float64) * 2.0 / HD)
    angles = (
        np.arange(SPAN, dtype=np.float32)[:, None] * inverse.astype(np.float32)[None, :]
    )
    angles = angles.astype(np.float64)
    return np.cos(angles).astype(np.float32), np.sin(angles).astype(np.float32)


def kv_lanes(part):
    low = list(range(16 * part, 16 * part + 16))
    return low + [64 + i for i in low] + list(range(128 + 32 * part, 160 + 32 * part))


def tables():
    cosine, sine = rope_tables()
    pack = np.zeros((2, 256, 512), np.float32)
    gather = np.zeros((4, 2, 128, 256), np.float32)
    bias_sel = np.zeros((4, 256, 128), np.float32)
    k_cos = np.ones((4, SPAN, 128), np.float32)
    k_sin = np.zeros((4, SPAN, 128), np.float32)
    turn = np.zeros((64, 64), np.float32)
    for lane in range(16):
        turn[lane + 16, lane] = 1.0
        turn[lane, lane + 16] = 1.0
    for part in range(4):
        lanes = kv_lanes(part)
        for lane, column in enumerate(lanes):
            pack[0, column, part * 128 + lane] = 1.0
            pack[1, column, part * 128 + 64 + lane] = 1.0
            gather[part, 0, lane, column] = 1.0
            gather[part, 1, 64 + lane, column] = 1.0
            bias_sel[part, column, lane] = 1.0
        bias_sel[part, :, 64:] = bias_sel[part, :, :64] @ turn
        dims = slice(16 * part, 16 * part + 16)
        for base in (0, 64):
            k_cos[part, :, base : base + 16] = cosine[:, dims]
            k_cos[part, :, base + 16 : base + 32] = cosine[:, dims]
            k_sin[part, :, base : base + 16] = -sine[:, dims]
            k_sin[part, :, base + 16 : base + 32] = sine[:, dims]
    unpack = np.zeros((128, 256), np.float32)
    unpack[:64, :64] = np.eye(64)
    unpack[:64, 64:128] = turn
    unpack[64:, 128:192] = np.eye(64)
    unpack[64:, 192:] = turn
    q_cos = np.concatenate([cosine, cosine], 1)
    q_sin = np.concatenate([-sine, sine], 1)
    return {
        "pack": jnp.asarray(pack, BF),
        "gather": jnp.asarray(gather, BF),
        "bias_sel": jnp.asarray(bias_sel, BF),
        "unpack": jnp.asarray(unpack, BF),
        "k_cos": jnp.asarray(k_cos),
        "k_sin": jnp.asarray(k_sin),
        "q_cos": jnp.asarray(q_cos),
        "q_sin": jnp.asarray(q_sin),
    }


def dot(a, b):
    return jnp.dot(a, b, preferred_element_type=F32)


VM = pl.BlockSpec(memory_space=pltpu.VMEM)
SM = pl.BlockSpec(memory_space=pltpu.SMEM)
AN = pl.BlockSpec(memory_space=pl.ANY)


def shape(dims, dtype=BF):
    return jax.ShapeDtypeStruct(dims, dtype)


def cost(mib):
    return pl.CostEstimate(flops=0, bytes_accessed=mib << 20, transcendentals=0)


def call(body, name, in_specs, out_shape, out_specs, estimate, scratch=(), after=(), mib=16):
    count = len(in_specs)

    def run(*refs):
        body(*refs[:count], *refs[count + len(after) :])

    kernel = pl.pallas_call(
        run,
        in_specs=in_specs + [AN] * len(after),
        out_specs=out_specs,
        out_shape=out_shape,
        scratch_shapes=list(scratch),
        compiler_params=pltpu.CompilerParams(vmem_limit_bytes=mib << 20),
        name=name,
        cost_estimate=estimate,
    )
    return lambda *args: kernel(*args, *after)


def pack_body(idx, w, gain, sel, out):
    row = gain[pl.ds((2 * idx[PAIR] + idx[SIDE]) * 16 + idx[TP] // 2, 1), :]
    lane = lax.broadcasted_iota(jnp.int32, (64, 128), 1)
    sub = lax.broadcasted_iota(jnp.int32, (64, 128), 0)
    hit = lane == sub + idx[TP] % 2 * 64
    scale = jnp.sum(jnp.where(hit, jnp.broadcast_to(row, (64, 128)), 0.0), axis=1, keepdims=True)
    for t in range(32):
        place = t // 8 * 4 + t % 4
        which = pl.ds((t // 4 + idx[Y_HI]) % 2, 1)
        for h in range(2):
            lanes = slice((2 * t + h) * 128, (2 * t + h + 1) * 128)
            block = (w[:, lanes].astype(F32) * scale).astype(BF)
            out[place, which, 32 + 64 * h : 96 + 64 * h, :] = block[None]
    for g in range(8):
        keys = w[:, 8192 + g * 128 : 8320 + g * 128]
        values = w[:, 9216 + g * 128 : 9344 + g * 128]
        both = (jnp.concatenate([keys, values], 1).astype(F32) * scale).astype(BF)
        packed = dot(both[:32], sel[0]) + dot(both[32:], sel[1])
        which = pl.ds((g + idx[Y_HI]) % 2, 1)
        for i in range(4):
            block = packed[:, i * 128 : (i + 1) * 128].astype(BF)
            out[g // 2 * 4 + i, which, :32, :] = block[None]


def pack(idx, w_qkv, gain, sel):
    return call(
        pack_body,
        "pack_weights",
        [SM, VM, VM, VM],
        shape((16, 2, 160, 128)),
        VM,
        cost(0),
    )(idx, w_qkv, gain, sel)


def cut_body(src, kv, q):
    kv[...] = src[:, 1, :32, :]
    q[...] = src[:, 0, 32:, :]


def cut_first(src, after):
    return call(
        cut_body,
        "cut_first",
        [VM],
        [shape((16, 32, 128)), shape((16, 128, 128))],
        [VM] * 2,
        cost(0),
        after=after,
    )(src)


def cut_q_body(src, q):
    q[...] = src[:, 1, 32:, :]


def cut_second(src, after):
    return call(
        cut_q_body, "cut_second", [VM], shape((16, 128, 128)), VM, cost(0), after=after
    )(src)


def near_body(lo, hi, src, got, out):
    out[0] = src[:, 0, lo:hi, :]
    out[1] = got[...]


def near_rows(lo, hi, src, got, after, name):
    return call(
        functools.partial(near_body, lo, hi),
        name,
        [VM, VM],
        shape((2, 16, hi - lo, 128)),
        VM,
        cost(0),
        after=after,
    )(src, got)


def row_groups(idx, own, mate, side, far):
    p, s, y = idx[PAIR], idx[SIDE], idx[Y_HI]
    for ref, core, here in ((own, p, s), (mate, 1 - p, s), (side, p, 1 - s), (far, 1 - p, 1 - s)):
        yield ref, 0, 2 * core + here, y
        yield ref, 1, 2 * core + 1 - here, 1 - y


BLOCKS = [pltpu.VMEM((4, 256, D), BF), pltpu.SemaphoreType.DMA((4,))]


def block_copy(x, buf, sem, i):
    return pltpu.make_async_copy(x.at[pl.ds(i * 256, 256)], buf.at[i], sem.at[i])


def start_blocks(x, buf, sem):
    for i in range(4):
        block_copy(x, buf, sem, i).start()


def project_block(x, buf, sem, ws, i, width):
    block_copy(x, buf, sem, i).wait()
    sums = None
    for j in range(4):
        w = ws[j].reshape(2048, width)
        part = dot(buf[i, :, j * 2048 : (j + 1) * 2048], w)
        sums = part if sums is None else sums + part
    return sums


def norm_body(idx, x, out, residual, buf, sem):
    columns = pl.ds(pl.multiple_of(idx[TP] * 256, 256), 256)
    copies = [
        pltpu.make_async_copy(x.at[pl.ds(i * 128, 128)], buf.at[i % 4], sem.at[i])
        for i in range(8)
    ]
    for copy in copies[:4]:
        copy.start()
    for i in range(8):
        copies[i].wait()
        rows = slice(i * 128, (i + 1) * 128)
        square = jnp.zeros((128, 128), F32)
        for c in range(64):
            piece = buf[i % 4, :, c * 128 : (c + 1) * 128].astype(F32)
            square += piece * piece
        mean = jnp.sum(square, axis=1, keepdims=True) * (1.0 / D)
        out[rows, :] = jnp.broadcast_to(lax.rsqrt(mean + 1e-6), (128, 128))
        residual[rows, :] = buf[i % 4, :, columns]
        if i < 4:
            copies[i + 4].start()


def norms(idx, x, after):
    return call(
        norm_body,
        "token_norms",
        [SM, AN],
        [shape((1024, 128), F32), shape((1024, 256))],
        [VM] * 2,
        cost(0),
        [pltpu.VMEM((4, 128, D), BF), pltpu.SemaphoreType.DMA((8,))],
        after,
        50,
    )(idx, x)


def kv_body(idx, x, own, mate, side, far, norm, unpack, bias, bsel, cos, sin, kv, ws, buf, sem):
    start_blocks(x, buf, sem)
    for ref, i, block, y in row_groups(idx, own, mate, side, far):
        both = dot(ref[i].reshape(512, 128), unpack[...]).astype(BF).reshape(4, 4, 32, 256)
        for z in range(4):
            ws[block, z, y, :, :32, :] = both[z, :, :, :128]
            ws[block, z, y, :, 32:, :] = both[z, :, :, 128:]
    g = idx[KV_HEAD]
    part = idx[X]
    base = jnp.concatenate([bias[pl.ds(64 + g, 1), :], bias[pl.ds(72 + g, 1), :]], 1)
    base = dot(jnp.broadcast_to(base, (8, 256)).astype(BF), bsel[part])[0:1]
    cosine = cos[part]
    sine = sin[part]
    lane = lax.broadcasted_iota(jnp.int32, (SPAN, 128), 1)
    for i in range(4):
        rows = slice(i * SPAN, (i + 1) * SPAN)
        sums = project_block(x, buf, sem, ws, i, 128) * norm[rows, :] + base
        turned = pltpu.roll(sums, 64, 1)
        place = slice((i % 2) * SPAN, (i % 2) * SPAN + SPAN)
        if i < 2:
            kv[place, :] = (sums * cosine + turned * sine).astype(BF)
        else:
            right = (turned * cosine + sums * sine).astype(BF)
            kv[place, :] = jnp.where(lane < 64, kv[place, :], right)


def keys_values(idx, x, ws, norm, tab, bias, after):
    return call(
        kv_body,
        "keys_values",
        [SM, AN] + [VM] * 10,
        shape((512, 128)),
        VM,
        cost(0),
        [
            pltpu.VMEM((4, 4, 2, 4, 64, 128), BF),
            *BLOCKS,
        ],
        after,
        50,
    )(
        idx, x, *ws, norm, tab["unpack"], bias, tab["bias_sel"], tab["k_cos"], tab["k_sin"]
    )


def join_body(idx, kv, first, second, gather, keys, values):
    for half in range(2):
        both = jnp.zeros((512, 256), F32)
        for k, piece in enumerate((kv, first, second.at[0], second.at[1])):
            both += dot(piece[...], gather[idx[X] ^ k, half])
        keys[half * 512 : (half + 1) * 512] = both[:, :128].astype(BF)
        values[half * 512 : (half + 1) * 512] = both[:, 128:].astype(BF)


def join_kv(idx, pieces, tab, after):
    return call(
        join_body,
        "join_keys_values",
        [SM] + [VM] * 4,
        [shape((1024, 128))] * 2,
        [VM] * 2,
        cost(0),
        after=after,
    )(idx, *pieces, tab["gather"])


def run_rows(ref, z):
    rows = [ref[4 * z : 4 * z + 4, 64 * h : 64 * h + 64, :].reshape(256, 128) for h in range(2)]
    return jnp.concatenate(rows, 1)


def half_block(x, ref, block, y):
    acc = None
    for z in range(4):
        start = pl.multiple_of(block * 2048 + z * 512 + y * 256, 256)
        term = dot(x[:, pl.ds(start, 256)], run_rows(ref, z))
        acc = term if acc is None else acc + term
    return acc


def early_body(idx, x, own, mate, side, far, got, got_mate, out, ws):
    p, s, y = idx[PAIR], idx[SIDE], idx[Y_HI]
    acc = half_block(x, own, 2 * p + s, y) + half_block(x, mate, 2 * (1 - p) + s, y)
    for k, (here, there) in enumerate(((side, got), (far, got_mate))):
        for z in range(4):
            ws[k, z, y] = run_rows(here, z)
            ws[k, z, 1 - y] = run_rows(there, z)
        core = p if k == 0 else 1 - p
        start = pl.multiple_of((2 * core + 1 - s) * 2048, 2048)
        acc += dot(x[:, pl.ds(start, 2048)], ws[k].reshape(2048, 256))
    out[...] = acc


def early_heads(idx, x, ws, after):
    return call(
        early_body,
        "project_early",
        [SM] + [VM] * 7,
        shape((1024, 256), F32),
        VM,
        cost(0),
        [pltpu.VMEM((2, 4, 2, 256, 256), BF)],
        after,
    )(idx, x, *ws)


def heads_body(
    idx, x, early, last, last_far, norm, bias, cos, sin, keys, values, first, second, acc
):
    p, s, y = idx[PAIR], idx[SIDE], 1 - idx[Y_HI]
    acc[...] = early[...] + half_block(x, last, 2 * p + s, y)
    acc[...] += half_block(x, last_far.at[0], 2 * (1 - p) + s, y)
    row = lax.broadcasted_iota(jnp.int32, (SPAN, SPAN), 0)
    col = lax.broadcasted_iota(jnp.int32, (SPAN, SPAN), 1)
    ones = jnp.ones((SPAN, HD), BF)
    for seq in range(4):
        rows = slice(seq * SPAN, (seq + 1) * SPAN)
        with_ones = jnp.concatenate([values[rows], ones], 1)
        for h in range(2):
            query = acc[rows, h * 128 : (h + 1) * 128] * norm[rows, :]
            query += bias[pl.ds(2 * idx[TP] + h, 1), :]
            query = (query * cos[...] + pltpu.roll(query, 64, 1) * sin[...]).astype(BF)
            scores = lax.dot_general(
                query, keys[rows], (((1,), (1,)), ((), ())), preferred_element_type=F32
            ) * (HD**-0.5)
            scores = jnp.where(row >= col, scores, -1e30)
            expo = jnp.exp(scores - jnp.max(scores, axis=1, keepdims=True)).astype(BF)
            mixed = dot(expo, with_ones)
            done = (mixed[:, :HD] / mixed[:, HD:]).astype(BF)
            (first, second)[h][rows, :] = done


def heads(idx, x, ws, norm, tab, bias, keys, values, after):
    return call(
        heads_body,
        "query_heads",
        [SM] + [VM] * 10,
        [shape((1024, 128))] * 2,
        [VM] * 2,
        cost(0),
        [pltpu.VMEM((1024, 256), F32)],
        after,
    )(idx, x, *ws, norm, bias, tab["q_cos"], tab["q_sin"], keys, values)


def beside_body(idx, att, across, out):
    same = idx[Y_HI] == idx[PAIR]
    out[:, :128] = jnp.where(same, att[...], across[...])
    out[:, 128:] = jnp.where(same, across[...], att[...])


def beside(idx, att, across, after):
    return call(
        beside_body,
        "beside",
        [SM, VM, VM],
        shape((1024, 256)),
        VM,
        cost(0),
        after=after,
    )(idx, att, across)


def stack_body(*refs):
    for i, ref in enumerate(refs[:-1]):
        refs[-1][i] = ref[...]


def stack(name, arrays, after):
    dims = (len(arrays),) + arrays[0].shape
    return call(
        stack_body,
        name,
        [VM] * len(arrays),
        shape(dims),
        VM,
        cost(0),
        after=after,
    )(*arrays)


def pick_body(idx, here, across, keep, send):
    p = idx[PAIR]
    for i, w in enumerate((here, across)):
        side = idx[SIDE] if i == 0 else 1 - idx[SIDE]
        keep[side] = w[pl.ds(pl.multiple_of(p * 1024, 1024), 1024), :]
        send[side] = w[pl.ds(pl.multiple_of((1 - p) * 1024, 1024), 1024), :]


def pick(idx, here, across, after):
    return call(
        pick_body,
        "pick_rows",
        [SM, VM, VM],
        [shape((2, 1024, 256))] * 2,
        [VM] * 2,
        cost(0),
        after=after,
    )(idx, here, across)


def route_body(idx, keep, recv, stay, leave):
    for r, out in enumerate((stay.at[0], stay.at[1], leave.at[0], leave.at[1])):
        goal = idx[Z] ^ r
        same = goal // 2 == idx[PAIR]

        @pl.when(same)
        def _():
            out[...] = keep[goal % 2]

        @pl.when(jnp.logical_not(same))
        def _():
            out[...] = recv[goal % 2]


def route(idx, keep, recv, after):
    return call(
        route_body,
        "route_rows",
        [SM, VM, VM],
        [shape((2, 1024, 256))] * 2,
        [VM] * 2,
        cost(0),
        after=after,
    )(idx, keep, recv)


def second_body(stay, came, out):
    out[0] = stay[1]
    out[1] = came[1]


def second_hop(stay, came, after):
    return call(
        second_body,
        "second_rows",
        [VM, VM],
        shape((2, 1024, 256)),
        VM,
        cost(0),
        after=after,
    )(stay, came)


def settle_body(idx, stay, came, last, out):
    z = idx[Z]
    out[z] = stay[0]
    out[z ^ 2] = came[0]
    out[z ^ 1] = last[0]
    out[z ^ 3] = last[1]


def settle(idx, stay, came, last, after):
    return call(
        settle_body,
        "settle_rows",
        [SM, VM, VM, VM],
        shape((4, 1024, 256)),
        VM,
        cost(0),
        after=after,
    )(idx, stay, came, last)


def w_rows(idx, own, other, r, part):
    z = (idx[Z] + 4 - r) % 4
    rows = []
    for h in range(2):
        for w in (own, other):
            rows.append(w[z, pl.ds(pl.multiple_of(part * 256 + h * 128, 128), 128), :])
    return jnp.concatenate(rows, 0)


def out_body(r, idx, h0, h1, h2, h3, there, a0, a1, a2, a3, own, other, out):
    same = idx[Y_HI] == idx[PAIR]
    acc = None
    for k, (here, both) in enumerate(zip((h0, h1, h2, h3), (a0, a1, a2, a3))):
        near = here[...]
        far = there[k]
        lanes = jnp.concatenate(
            [jnp.where(same, near, far), jnp.where(same, far, near), both[...]], 1
        )
        term = dot(lanes, w_rows(idx, own, other, r, (idx[X] + 4 - k) % 4))
        acc = term if acc is None else acc + term
    out[...] = acc.astype(BF)


def project_out(r, idx, here, there, both, own, other, after):
    return call(
        functools.partial(out_body, r),
        f"project_out_{r}",
        [SM] + [VM] * 11,
        shape((1024, 256)),
        VM,
        cost(0),
        after=after,
    )(idx, *here, there, *both, own, other)


def finish_body(residual, p0, p1, p2, p3, out):
    total = residual[...].astype(F32)
    for part in (p0, p1, p2, p3):
        total += part[...].astype(F32)
    out[...] = total.astype(BF)


def finish(residual, parts):
    return call(
        finish_body, "add_residual", [VM] * 5, shape((1024, 256)), VM, cost(0)
    )(residual, *parts)


SWAP = [(0, 1), (1, 0)]


def shift(dz, dy, dx):
    return [
        (
            z * 8 + y * 4 + x,
            (z + dz) % 4 * 8 + (y + dy) % 2 * 4 + (x + dx) % 4,
        )
        for z in range(4)
        for y in range(2)
        for x in range(4)
    ]


def flip(bits):
    return [(t, t ^ bits) for t in range(32)]


PLANES = [[z * 8 + y * 4 + x for z in range(4) for x in range(4)] for y in range(2)]
DIAGONAL = [
    (s * 32 + t, (1 - s) * 32 + (t ^ 4)) for s in range(2) for t in range(32)
]


def shards(tokens, norm_gain, w_qkv, qkv_bias, w_out):
    tab = tables()
    seqs, span, width = tokens.shape
    p = lax.axis_index("pair")
    s = lax.axis_index("side")
    t = lax.axis_index("tp")
    idx = jnp.stack([t, t // 4, t % 4, p, t // 4 % 2, t // 8, s]).astype(jnp.int32)
    bias = qkv_bias.reshape(80, 128).astype(F32)
    x = tokens.reshape(seqs * span, width)

    w_across = lax.ppermute(w_out, "side", SWAP)
    packed = pack(idx, w_qkv, norm_gain.reshape(64, 128), tab["pack"])
    blocks = lax.all_to_all(
        packed, "tp", split_axis=0, concat_axis=0, tiled=True, axis_index_groups=PLANES
    )
    norm, residual = norms(idx, x, [packed])
    keep, send = pick(idx, w_out, w_across, [norm])
    kv_other, q_own = cut_first(blocks, [keep])
    q_side = lax.ppermute(q_own, "side", SWAP)
    kv_got = lax.ppermute(kv_other, ("side", "tp"), DIAGONAL)
    kv_own = near_rows(0, 32, blocks, kv_got, [q_own], "near_kv")
    kv_side = lax.ppermute(kv_own, "side", SWAP)
    kv_mate = lax.ppermute(kv_own, "pair", SWAP)
    q_got = lax.ppermute(cut_second(blocks, [kv_own]), ("side", "tp"), DIAGONAL)
    stay, leave = route(idx, keep, lax.ppermute(send, "pair", SWAP), [kv_own])
    kv_far = lax.ppermute(kv_side, "pair", SWAP)
    kv_piece = keys_values(
        idx, x, (kv_own, kv_mate, kv_side, kv_far), norm, tab, bias, [q_got, stay]
    )
    got_side = lax.ppermute(q_got, "side", SWAP)
    q_mates = [lax.ppermute(q, "pair", SWAP) for q in (q_own, q_side, q_got)]
    first = lax.ppermute(kv_piece, "tp", flip(1))
    pieces = stack("stack_kv", [kv_piece, first], [*q_mates, got_side])
    second = lax.ppermute(pieces, "tp", flip(2))
    came = lax.ppermute(leave, "tp", flip(16))
    hop = second_hop(stay, came, [pieces])
    late = stack("late_q", [got_side], [hop])
    early = early_heads(
        idx, x, (q_own, q_mates[0], q_side, q_mates[1], q_got, q_mates[2]), [late]
    )
    keys, values = join_kv(idx, (kv_piece, first, second), tab, [early])
    ws = (early, got_side, lax.ppermute(late, "pair", SWAP).reshape(1, 16, 128, 128))
    att0, att1 = heads(idx, x, ws, norm, tab, bias, keys, values, [])
    here = [att0] + [lax.ppermute(att0, "tp", shift(0, 0, r)) for r in range(1, 4)]
    stacked = stack("stack_head0", here, [])
    there = lax.ppermute(stacked, "tp", shift(0, 1, 0))
    both = beside(idx, att1, lax.ppermute(att1, "tp", shift(0, 1, 0)), [stacked])
    plane = [both] + [lax.ppermute(both, "tp", shift(0, 0, r)) for r in range(1, 4)]
    w_own = settle(idx, stay, came, lax.ppermute(hop, "tp", flip(8)), [both])
    w_other = lax.ppermute(w_own, "pair", SWAP)

    parts = []
    for r in (2, 1, 3, 0):
        partial = project_out(r, idx, here, there, plane, w_own, w_other, parts[-1:])
        parts.append(partial)
    parts = [
        lax.ppermute(part, "tp", shift(-r, 0, 0)) if r else part
        for r, part in zip((2, 1, 3, 0), parts)
    ]
    return finish(residual, parts).reshape(seqs, span, 256)


def solution(mesh):
    placed = (
        P(("pair", "side"), None, None),
        P(),
        P(("pair", "side", "tp"), None),
        P(),
        P(("pair", "side"), "tp"),
    )
    return jax.shard_map(
        shards,
        mesh=mesh,
        in_specs=placed,
        out_specs=P(("pair", "side"), None, "tp"),
        check_vma=False,
    )
```

```python
import functools

import jax
import jax.numpy as jnp
import numpy as np
from jax import lax
from jax.experimental import pallas as pl
from jax.experimental.pallas import tpu as pltpu
from jax.sharding import PartitionSpec as P

HD = 128
SPAN = 256
D = 8192
BF = jnp.bfloat16
F32 = jnp.float32
TP, KV_HEAD, X, PAIR, Y_HI, Z, SIDE = range(7)


def rope_tables():
    half = HD // 2
    inverse = 1000000.0 ** (-np.arange(half, dtype=np.float64) * 2.0 / HD)
    angles = (
        np.arange(SPAN, dtype=np.float32)[:, None] * inverse.astype(np.float32)[None, :]
    )
    angles = angles.astype(np.float64)
    return np.cos(angles).astype(np.float32), np.sin(angles).astype(np.float32)


def kv_lanes(part):
    low = list(range(16 * part, 16 * part + 16))
    return low + [64 + i for i in low] + list(range(128 + 32 * part, 160 + 32 * part))


def tables():
    cosine, sine = rope_tables()
    pack = np.zeros((2, 256, 512), np.float32)
    gather = np.zeros((4, 2, 128, 256), np.float32)
    bias_sel = np.zeros((4, 256, 128), np.float32)
    k_cos = np.ones((4, SPAN, 128), np.float32)
    k_sin = np.zeros((4, SPAN, 128), np.float32)
    turn = np.zeros((64, 64), np.float32)
    for lane in range(16):
        turn[lane + 16, lane] = 1.0
        turn[lane, lane + 16] = 1.0
    for part in range(4):
        lanes = kv_lanes(part)
        for lane, column in enumerate(lanes):
            pack[0, column, part * 128 + lane] = 1.0
            pack[1, column, part * 128 + 64 + lane] = 1.0
            gather[part, 0, lane, column] = 1.0
            gather[part, 1, 64 + lane, column] = 1.0
            bias_sel[part, column, lane] = 1.0
        bias_sel[part, :, 64:] = bias_sel[part, :, :64] @ turn
        dims = slice(16 * part, 16 * part + 16)
        for base in (0, 64):
            k_cos[part, :, base : base + 16] = cosine[:, dims]
            k_cos[part, :, base + 16 : base + 32] = cosine[:, dims]
            k_sin[part, :, base : base + 16] = -sine[:, dims]
            k_sin[part, :, base + 16 : base + 32] = sine[:, dims]
    unpack = np.zeros((128, 256), np.float32)
    unpack[:64, :64] = np.eye(64)
    unpack[:64, 64:128] = turn
    unpack[64:, 128:192] = np.eye(64)
    unpack[64:, 192:] = turn
    q_cos = np.concatenate([cosine, cosine], 1)
    q_sin = np.concatenate([-sine, sine], 1)
    return {
        "pack": jnp.asarray(pack, BF),
        "gather": jnp.asarray(gather, BF),
        "bias_sel": jnp.asarray(bias_sel, BF),
        "unpack": jnp.asarray(unpack, BF),
        "k_cos": jnp.asarray(k_cos),
        "k_sin": jnp.asarray(k_sin),
        "q_cos": jnp.asarray(q_cos),
        "q_sin": jnp.asarray(q_sin),
    }


def dot(a, b):
    return jnp.dot(a, b, preferred_element_type=F32)


VM = pl.BlockSpec(memory_space=pltpu.VMEM)
SM = pl.BlockSpec(memory_space=pltpu.SMEM)
AN = pl.BlockSpec(memory_space=pl.ANY)


def shape(dims, dtype=BF):
    return jax.ShapeDtypeStruct(dims, dtype)


def cost(mib):
    return pl.CostEstimate(flops=0, bytes_accessed=mib << 20, transcendentals=0)


def call(body, name, in_specs, out_shape, out_specs, estimate, scratch=(), after=(), mib=16):
    count = len(in_specs)

    def run(*refs):
        body(*refs[:count], *refs[count + len(after) :])

    kernel = pl.pallas_call(
        run,
        in_specs=in_specs + [AN] * len(after),
        out_specs=out_specs,
        out_shape=out_shape,
        scratch_shapes=list(scratch),
        compiler_params=pltpu.CompilerParams(vmem_limit_bytes=mib << 20),
        name=name,
        cost_estimate=estimate,
    )
    return lambda *args: kernel(*args, *after)


def pack_body(idx, w, gain, sel, out):
    row = gain[pl.ds((2 * idx[PAIR] + idx[SIDE]) * 16 + idx[TP] // 2, 1), :]
    lane = lax.broadcasted_iota(jnp.int32, (64, 128), 1)
    sub = lax.broadcasted_iota(jnp.int32, (64, 128), 0)
    hit = lane == sub + idx[TP] % 2 * 64
    scale = jnp.sum(jnp.where(hit, jnp.broadcast_to(row, (64, 128)), 0.0), axis=1, keepdims=True)
    for t in range(32):
        place = t // 8 * 4 + t % 4
        which = pl.ds((t // 4 + idx[Y_HI]) % 2, 1)
        for h in range(2):
            lanes = slice((2 * t + h) * 128, (2 * t + h + 1) * 128)
            block = (w[:, lanes].astype(F32) * scale).astype(BF)
            out[place, which, 32 + 64 * h : 96 + 64 * h, :] = block[None]
    for g in range(8):
        keys = w[:, 8192 + g * 128 : 8320 + g * 128]
        values = w[:, 9216 + g * 128 : 9344 + g * 128]
        both = (jnp.concatenate([keys, values], 1).astype(F32) * scale).astype(BF)
        packed = dot(both[:32], sel[0]) + dot(both[32:], sel[1])
        which = pl.ds((g + idx[Y_HI]) % 2, 1)
        for i in range(4):
            block = packed[:, i * 128 : (i + 1) * 128].astype(BF)
            out[g // 2 * 4 + i, which, :32, :] = block[None]


def pack(idx, w_qkv, gain, sel):
    return call(
        pack_body,
        "pack_weights",
        [SM, VM, VM, VM],
        shape((16, 2, 160, 128)),
        VM,
        cost(0),
    )(idx, w_qkv, gain, sel)


def cut_body(src, kv, q):
    kv[...] = src[:, 1, :32, :]
    q[...] = src[:, 0, 32:, :]


def cut_first(src, after):
    return call(
        cut_body,
        "cut_first",
        [VM],
        [shape((16, 32, 128)), shape((16, 128, 128))],
        [VM] * 2,
        cost(0),
        after=after,
    )(src)


def cut_q_body(src, q):
    q[...] = src[:, 1, 32:, :]


def cut_second(src, after):
    return call(
        cut_q_body, "cut_second", [VM], shape((16, 128, 128)), VM, cost(0), after=after
    )(src)


def near_body(lo, hi, src, got, out):
    out[0] = src[:, 0, lo:hi, :]
    out[1] = got[...]


def near_rows(lo, hi, src, got, after, name):
    return call(
        functools.partial(near_body, lo, hi),
        name,
        [VM, VM],
        shape((2, 16, hi - lo, 128)),
        VM,
        cost(0),
        after=after,
    )(src, got)


def row_groups(idx, own, mate, side, far):
    p, s, y = idx[PAIR], idx[SIDE], idx[Y_HI]
    for ref, core, here in ((own, p, s), (mate, 1 - p, s), (side, p, 1 - s), (far, 1 - p, 1 - s)):
        yield ref, 0, 2 * core + here, y
        yield ref, 1, 2 * core + 1 - here, 1 - y


def norm_body(idx, x, out, residual, buf, sem):
    columns = pl.ds(pl.multiple_of(idx[TP] * 256, 256), 256)
    copies = [
        pltpu.make_async_copy(x.at[pl.ds(i * 128, 128)], buf.at[i % 4], sem.at[i])
        for i in range(8)
    ]
    for copy in copies[:4]:
        copy.start()
    for i in range(8):
        copies[i].wait()
        rows = slice(i * 128, (i + 1) * 128)
        square = jnp.zeros((128, 128), F32)
        for c in range(64):
            piece = buf[i % 4, :, c * 128 : (c + 1) * 128].astype(F32)
            square += piece * piece
        mean = jnp.sum(square, axis=1, keepdims=True) * (1.0 / D)
        out[rows, :] = jnp.broadcast_to(lax.rsqrt(mean + 1e-6), (128, 128))
        residual[rows, :] = buf[i % 4, :, columns]
        if i < 4:
            copies[i + 4].start()


def norms(idx, x, after):
    return call(
        norm_body,
        "token_norms",
        [SM, AN],
        [shape((1024, 128), F32), shape((1024, 256))],
        [VM] * 2,
        cost(0),
        [pltpu.VMEM((4, 128, D), BF), pltpu.SemaphoreType.DMA((8,))],
        after,
        50,
    )(idx, x)


def kv_sums(idx, x, groups, unpack, ws):
    acc = None
    for k, (ref, i, block, y) in enumerate(groups):
        both = dot(ref[i].reshape(512, 128), unpack[...]).astype(BF).reshape(4, 4, 32, 256)
        for z in range(4):
            ws[k, z, :, :32, :] = both[z, :, :, :128]
            ws[k, z, :, 32:, :] = both[z, :, :, 128:]
        for z in range(4):
            start = pl.multiple_of(block * 2048 + z * 512 + y * 256, 256)
            term = dot(x[:, pl.ds(start, 256)], ws[k, z].reshape(256, 128))
            acc = term if acc is None else acc + term
    return acc


def kv_early_body(idx, x, own, mate, unpack, out, ws):
    groups = list(row_groups(idx, own, mate, own, mate))[:4]
    out[...] = kv_sums(idx, x, groups, unpack, ws)


def kv_body(idx, x, early, side, far, norm, unpack, bias, bsel, cos, sin, kv, ws):
    groups = list(row_groups(idx, side, far, side, far))[4:]
    acc = early[...] + kv_sums(idx, x, groups, unpack, ws)
    g = idx[KV_HEAD]
    part = idx[X]
    base = jnp.concatenate([bias[pl.ds(64 + g, 1), :], bias[pl.ds(72 + g, 1), :]], 1)
    base = dot(jnp.broadcast_to(base, (8, 256)).astype(BF), bsel[part])[0:1]
    cosine = cos[part]
    sine = sin[part]
    acc = acc * norm[...] + base
    lane = lax.broadcasted_iota(jnp.int32, (SPAN, 128), 1)
    for i in range(2):
        a = acc[i * 256 : (i + 1) * 256]
        b = acc[512 + i * 256 : 512 + (i + 1) * 256]
        left = a * cosine + pltpu.roll(a, 64, 1) * sine
        right = pltpu.roll(b, 64, 1) * cosine + b * sine
        kv[i * 256 : (i + 1) * 256] = jnp.where(lane < 64, left, right).astype(BF)


KV_ROWS = pltpu.VMEM((4, 4, 4, 64, 128), BF)


def early_keys_values(idx, x, ws, tab, after):
    return call(
        kv_early_body,
        "keys_values_early",
        [SM] + [VM] * 4,
        shape((1024, 128), F32),
        VM,
        cost(0),
        [KV_ROWS],
        after,
    )(idx, x, *ws, tab["unpack"])


def keys_values(idx, x, ws, norm, tab, bias, after):
    return call(
        kv_body,
        "keys_values",
        [SM] + [VM] * 10,
        shape((512, 128)),
        VM,
        cost(0),
        [KV_ROWS],
        after,
    )(
        idx, x, *ws, norm, tab["unpack"], bias, tab["bias_sel"], tab["k_cos"], tab["k_sin"]
    )


def join_body(idx, p0, p1, p2, p3, gather, keys, values):
    for half in range(2):
        both = jnp.zeros((512, 256), F32)
        for k, piece in enumerate((p0, p1, p2, p3)):
            both += dot(piece[...], gather[(idx[X] + 4 - k) % 4, half])
        keys[half * 512 : (half + 1) * 512] = both[:, :128].astype(BF)
        values[half * 512 : (half + 1) * 512] = both[:, 128:].astype(BF)


def join_kv(idx, pieces, tab, after):
    return call(
        join_body,
        "join_keys_values",
        [SM] + [VM] * 5,
        [shape((1024, 128))] * 2,
        [VM] * 2,
        cost(0),
        after=after,
    )(idx, *pieces, tab["gather"])


def run_rows(ref, z):
    rows = [ref[4 * z : 4 * z + 4, 64 * h : 64 * h + 64, :].reshape(256, 128) for h in range(2)]
    return jnp.concatenate(rows, 1)


def half_block(x, ref, block, y):
    acc = None
    for z in range(4):
        start = pl.multiple_of(block * 2048 + z * 512 + y * 256, 256)
        term = dot(x[:, pl.ds(start, 256)], run_rows(ref, z))
        acc = term if acc is None else acc + term
    return acc


def early_body(idx, x, own, mate, both, mates, out, ws):
    p, s, y = idx[PAIR], idx[SIDE], idx[Y_HI]
    acc = half_block(x, own, 2 * p + s, y) + half_block(x, mate, 2 * (1 - p) + s, y)
    for k, rows in enumerate((both, mates)):
        for z in range(4):
            ws[k, z, y] = run_rows(rows.at[0], z)
            ws[k, z, 1 - y] = run_rows(rows.at[1], z)
        core = p if k == 0 else 1 - p
        start = pl.multiple_of((2 * core + 1 - s) * 2048, 2048)
        acc += dot(x[:, pl.ds(start, 2048)], ws[k].reshape(2048, 256))
    out[...] = acc


def early_heads(idx, x, ws, after):
    return call(
        early_body,
        "project_early",
        [SM] + [VM] * 5,
        shape((1024, 256), F32),
        VM,
        cost(0),
        [pltpu.VMEM((2, 4, 2, 256, 256), BF)],
        after,
    )(idx, x, *ws)


def heads_body(
    idx, x, early, last, last_far, norm, bias, cos, sin, keys, values, first, second, acc
):
    p, s, y = idx[PAIR], idx[SIDE], 1 - idx[Y_HI]
    acc[...] = early[...] + half_block(x, last, 2 * p + s, y)
    acc[...] += half_block(x, last_far.at[0], 2 * (1 - p) + s, y)
    row = lax.broadcasted_iota(jnp.int32, (SPAN, SPAN), 0)
    col = lax.broadcasted_iota(jnp.int32, (SPAN, SPAN), 1)
    ones = jnp.ones((SPAN, HD), BF)
    for seq in range(4):
        rows = slice(seq * SPAN, (seq + 1) * SPAN)
        with_ones = jnp.concatenate([values[rows], ones], 1)
        for h in range(2):
            query = acc[rows, h * 128 : (h + 1) * 128] * norm[rows, :]
            query += bias[pl.ds(2 * idx[TP] + h, 1), :]
            query = (query * cos[...] + pltpu.roll(query, 64, 1) * sin[...]).astype(BF)
            scores = lax.dot_general(
                query, keys[rows], (((1,), (1,)), ((), ())), preferred_element_type=F32
            ) * (HD**-0.5)
            scores = jnp.where(row >= col, scores, -1e30)
            expo = jnp.exp(scores - jnp.max(scores, axis=1, keepdims=True)).astype(BF)
            mixed = dot(expo, with_ones)
            done = (mixed[:, :HD] / mixed[:, HD:]).astype(BF)
            (first, second)[h][rows, :] = done


def heads(idx, x, ws, norm, tab, bias, keys, values, after):
    return call(
        heads_body,
        "query_heads",
        [SM] + [VM] * 10,
        [shape((1024, 128))] * 2,
        [VM] * 2,
        cost(0),
        [pltpu.VMEM((1024, 256), F32)],
        after,
    )(idx, x, *ws, norm, bias, tab["q_cos"], tab["q_sin"], keys, values)


def beside_body(idx, att, across, out):
    same = idx[Y_HI] == idx[PAIR]
    out[:, :128] = jnp.where(same, att[...], across[...])
    out[:, 128:] = jnp.where(same, across[...], att[...])


def beside(idx, att, across, after):
    return call(
        beside_body,
        "beside",
        [SM, VM, VM],
        shape((1024, 256)),
        VM,
        cost(0),
        after=after,
    )(idx, att, across)


def stack_body(*refs):
    for i, ref in enumerate(refs[:-1]):
        refs[-1][i] = ref[...]


def stack(name, arrays, after):
    dims = (len(arrays),) + arrays[0].shape
    return call(
        stack_body,
        name,
        [VM] * len(arrays),
        shape(dims),
        VM,
        cost(0),
        after=after,
    )(*arrays)


def pick_body(idx, here, across, keep, send):
    p = idx[PAIR]
    for i, w in enumerate((here, across)):
        side = idx[SIDE] if i == 0 else 1 - idx[SIDE]
        keep[side] = w[pl.ds(pl.multiple_of(p * 1024, 1024), 1024), :]
        send[side] = w[pl.ds(pl.multiple_of((1 - p) * 1024, 1024), 1024), :]


def pick(idx, here, across, after):
    return call(
        pick_body,
        "pick_rows",
        [SM, VM, VM],
        [shape((2, 1024, 256))] * 2,
        [VM] * 2,
        cost(0),
        after=after,
    )(idx, here, across)


def route_body(idx, keep, recv, stay, leave):
    for r, out in enumerate((stay.at[0], stay.at[1], leave.at[0], leave.at[1])):
        goal = idx[Z] ^ r
        same = goal // 2 == idx[PAIR]

        @pl.when(same)
        def _():
            out[...] = keep[goal % 2]

        @pl.when(jnp.logical_not(same))
        def _():
            out[...] = recv[goal % 2]


def route(idx, keep, recv, after):
    return call(
        route_body,
        "route_rows",
        [SM, VM, VM],
        [shape((2, 1024, 256))] * 2,
        [VM] * 2,
        cost(0),
        after=after,
    )(idx, keep, recv)


def second_body(stay, came, near, out):
    near[0] = stay[0]
    near[1] = came[0]
    out[0] = stay[1]
    out[1] = came[1]


def second_hop(stay, came, after):
    return call(
        second_body,
        "second_rows",
        [VM, VM],
        [shape((2, 1024, 256))] * 2,
        [VM] * 2,
        cost(0),
        after=after,
    )(stay, came)


def w_rows(w, other, i, part):
    rows = []
    for h in range(2):
        for ref in (w, other):
            rows.append(ref[i, pl.ds(pl.multiple_of(part * 256 + h * 128, 128), 128), :])
    return jnp.concatenate(rows, 0)


def out_body(r, idx, h0, h1, h2, h3, there, a0, a1, a2, a3, own, other, out):
    same = idx[Y_HI] == idx[PAIR]
    i = r // 2 if r % 2 == 0 else (idx[Z] + (r + 1) // 2) % 2
    acc = None
    for k, (here, both) in enumerate(zip((h0, h1, h2, h3), (a0, a1, a2, a3))):
        near = here[...]
        far = there[k]
        lanes = jnp.concatenate(
            [jnp.where(same, near, far), jnp.where(same, far, near), both[...]], 1
        )
        term = dot(lanes, w_rows(own, other, i, (idx[X] + 4 - k) % 4))
        acc = term if acc is None else acc + term
    out[...] = acc.astype(BF)


def project_out(r, idx, here, there, both, own, other, after):
    return call(
        functools.partial(out_body, r),
        f"project_out_{r}",
        [SM] + [VM] * 11,
        shape((1024, 256)),
        VM,
        cost(0),
        after=after,
    )(idx, *here, there, *both, own, other)


def finish_body(residual, p0, p1, p2, p3, out):
    total = residual[...].astype(F32)
    for part in (p0, p1, p2, p3):
        total += part[...].astype(F32)
    out[...] = total.astype(BF)


def finish(residual, parts):
    return call(
        finish_body, "add_residual", [VM] * 5, shape((1024, 256)), VM, cost(0)
    )(residual, *parts)


SWAP = [(0, 1), (1, 0)]


def shift(dz, dy, dx):
    return [
        (
            z * 8 + y * 4 + x,
            (z + dz) % 4 * 8 + (y + dy) % 2 * 4 + (x + dx) % 4,
        )
        for z in range(4)
        for y in range(2)
        for x in range(4)
    ]


def flip(bits):
    return [(t, t ^ bits) for t in range(32)]


PLANES = [[z * 8 + y * 4 + x for z in range(4) for x in range(4)] for y in range(2)]
DIAGONAL = [
    (s * 32 + t, (1 - s) * 32 + (t ^ 4)) for s in range(2) for t in range(32)
]


def shards(tokens, norm_gain, w_qkv, qkv_bias, w_out):
    tab = tables()
    seqs, span, width = tokens.shape
    p = lax.axis_index("pair")
    s = lax.axis_index("side")
    t = lax.axis_index("tp")
    idx = jnp.stack([t, t // 4, t % 4, p, t // 4 % 2, t // 8, s]).astype(jnp.int32)
    bias = qkv_bias.reshape(80, 128).astype(F32)
    x = tokens.reshape(seqs * span, width)

    w_across = lax.ppermute(w_out, "side", SWAP)
    packed = pack(idx, w_qkv, norm_gain.reshape(64, 128), tab["pack"])
    blocks = lax.all_to_all(
        packed, "tp", split_axis=0, concat_axis=0, tiled=True, axis_index_groups=PLANES
    )
    norm, residual = norms(idx, x, [packed])
    keep, send = pick(idx, w_out, w_across, [norm])
    kv_other, q_own = cut_first(blocks, [keep])
    q_side = lax.ppermute(q_own, "side", SWAP)
    kv_got = lax.ppermute(kv_other, ("side", "tp"), DIAGONAL)
    stay, leave = route(idx, keep, lax.ppermute(send, "pair", SWAP), [q_own])
    kv_own = near_rows(0, 32, blocks, kv_got, [stay], "near_kv")
    kv_side = lax.ppermute(kv_own, "side", SWAP)
    kv_mate = lax.ppermute(kv_own, "pair", SWAP)
    q_other = cut_second(blocks, [kv_own])
    q_got = lax.ppermute(q_other, ("side", "tp"), DIAGONAL)
    kv_early = early_keys_values(idx, x, (kv_own, kv_mate), tab, [q_other])
    kv_late = stack("late_kv", [kv_side], [kv_early])
    kv_far = lax.ppermute(kv_late, "pair", SWAP).reshape(kv_side.shape)
    q_mate = lax.ppermute(q_own, "pair", SWAP)
    q_both = stack("late_queries", [q_side, q_got], [kv_late])
    q_mates = lax.ppermute(q_both, "pair", SWAP)
    kv_piece = keys_values(
        idx, x, (kv_early, kv_side, kv_far), norm, tab, bias, [q_mate, q_mates]
    )
    got_side = lax.ppermute(q_got, "side", SWAP)
    pieces = [kv_piece] + [
        lax.ppermute(kv_piece, "tp", shift(0, 0, r)) for r in range(1, 4)
    ]
    came = lax.ppermute(leave, "tp", flip(16))
    early = early_heads(
        idx,
        x,
        (q_own, q_mate, q_both, q_mates),
        [kv_piece],
    )
    late = stack("late_q", [got_side], [early, pieces[1], pieces[3]])
    keys, values = join_kv(idx, pieces, tab, [late])
    late_far = lax.ppermute(late, "pair", SWAP)
    ws = (early, got_side, late_far)
    att0, att1 = heads(idx, x, ws, norm, tab, bias, keys, values, [])
    near, hop = second_hop(stay, came, [att0])
    near_other = lax.ppermute(near, "pair", SWAP)
    last = lax.ppermute(hop, "tp", flip(8))
    last_other = lax.ppermute(last, "pair", SWAP)
    here = [att0] + [lax.ppermute(att0, "tp", shift(0, 0, r)) for r in range(1, 4)]
    stacked = stack("stack_head0", here, [near])
    there = lax.ppermute(stacked, "tp", shift(0, 1, 0))
    both = beside(idx, att1, lax.ppermute(att1, "tp", shift(0, 1, 0)), [stacked])
    plane = [both] + [lax.ppermute(both, "tp", shift(0, 0, r)) for r in range(1, 4)]

    parts = []
    for r in (2, 1, 3, 0):
        w, w_other = (last, last_other) if r % 2 else (near, near_other)
        parts.append(
            project_out(r, idx, here, there, plane, w, w_other, [both, *parts[-1:]])
        )
    parts = [
        lax.ppermute(part, "tp", shift(-r, 0, 0)) if r else part
        for r, part in zip((2, 1, 3, 0), parts)
    ]
    return finish(residual, parts).reshape(seqs, span, 256)


def solution(mesh):
    placed = (
        P(("pair", "side"), None, None),
        P(),
        P(("pair", "side", "tp"), None),
        P(),
        P(("pair", "side"), "tp"),
    )
    return jax.shard_map(
        shards,
        mesh=mesh,
        in_specs=placed,
        out_specs=P(("pair", "side"), None, "tp"),
        check_vma=False,
    )
```

```python
import functools

import jax
import jax.numpy as jnp
import numpy as np
from jax import lax
from jax.experimental import pallas as pl
from jax.experimental.pallas import tpu as pltpu
from jax.sharding import PartitionSpec as P

HD = 128
SPAN = 256
D = 8192
BF = jnp.bfloat16
F32 = jnp.float32
TP, KV_HEAD, X, PAIR, Y_HI, Z, SIDE = range(7)


def rope_tables():
    half = HD // 2
    inverse = 1000000.0 ** (-np.arange(half, dtype=np.float64) * 2.0 / HD)
    angles = (
        np.arange(SPAN, dtype=np.float32)[:, None] * inverse.astype(np.float32)[None, :]
    )
    angles = angles.astype(np.float64)
    return np.cos(angles).astype(np.float32), np.sin(angles).astype(np.float32)


def kv_lanes(part):
    low = list(range(16 * part, 16 * part + 16))
    return low + [64 + i for i in low] + list(range(128 + 32 * part, 160 + 32 * part))


def tables():
    cosine, sine = rope_tables()
    pack = np.zeros((2, 256, 512), np.float32)
    gather = np.zeros((4, 2, 128, 256), np.float32)
    bias_sel = np.zeros((4, 256, 128), np.float32)
    k_cos = np.ones((4, SPAN, 128), np.float32)
    k_sin = np.zeros((4, SPAN, 128), np.float32)
    turn = np.zeros((64, 64), np.float32)
    for lane in range(16):
        turn[lane + 16, lane] = 1.0
        turn[lane, lane + 16] = 1.0
    for part in range(4):
        lanes = kv_lanes(part)
        for lane, column in enumerate(lanes):
            pack[0, column, part * 128 + lane] = 1.0
            pack[1, column, part * 128 + 64 + lane] = 1.0
            gather[part, 0, lane, column] = 1.0
            gather[part, 1, 64 + lane, column] = 1.0
            bias_sel[part, column, lane] = 1.0
        bias_sel[part, :, 64:] = bias_sel[part, :, :64] @ turn
        dims = slice(16 * part, 16 * part + 16)
        for base in (0, 64):
            k_cos[part, :, base : base + 16] = cosine[:, dims]
            k_cos[part, :, base + 16 : base + 32] = cosine[:, dims]
            k_sin[part, :, base : base + 16] = -sine[:, dims]
            k_sin[part, :, base + 16 : base + 32] = sine[:, dims]
    unpack = np.zeros((128, 256), np.float32)
    unpack[:64, :64] = np.eye(64)
    unpack[:64, 64:128] = turn
    unpack[64:, 128:192] = np.eye(64)
    unpack[64:, 192:] = turn
    q_cos = np.concatenate([cosine, cosine], 1)
    q_sin = np.concatenate([-sine, sine], 1)
    return {
        "pack": jnp.asarray(pack, BF),
        "gather": jnp.asarray(gather, BF),
        "bias_sel": jnp.asarray(bias_sel, BF),
        "unpack": jnp.asarray(unpack, BF),
        "k_cos": jnp.asarray(k_cos),
        "k_sin": jnp.asarray(k_sin),
        "q_cos": jnp.asarray(q_cos),
        "q_sin": jnp.asarray(q_sin),
    }


def dot(a, b):
    return jnp.dot(a, b, preferred_element_type=F32)


VM = pl.BlockSpec(memory_space=pltpu.VMEM)
SM = pl.BlockSpec(memory_space=pltpu.SMEM)
AN = pl.BlockSpec(memory_space=pl.ANY)


def shape(dims, dtype=BF):
    return jax.ShapeDtypeStruct(dims, dtype)


def cost(mib):
    return pl.CostEstimate(flops=0, bytes_accessed=mib << 20, transcendentals=0)


def call(body, name, in_specs, out_shape, out_specs, estimate, scratch=(), after=(), mib=16):
    count = len(in_specs)

    def run(*refs):
        body(*refs[:count], *refs[count + len(after) :])

    kernel = pl.pallas_call(
        run,
        in_specs=in_specs + [AN] * len(after),
        out_specs=out_specs,
        out_shape=out_shape,
        scratch_shapes=list(scratch),
        compiler_params=pltpu.CompilerParams(vmem_limit_bytes=mib << 20),
        name=name,
        cost_estimate=estimate,
    )
    return lambda *args: kernel(*args, *after)


def pack_body(idx, w, gain, sel, out):
    row = gain[pl.ds((2 * idx[PAIR] + idx[SIDE]) * 16 + idx[TP] // 2, 1), :]
    lane = lax.broadcasted_iota(jnp.int32, (64, 128), 1)
    sub = lax.broadcasted_iota(jnp.int32, (64, 128), 0)
    hit = lane == sub + idx[TP] % 2 * 64
    scale = jnp.sum(jnp.where(hit, jnp.broadcast_to(row, (64, 128)), 0.0), axis=1, keepdims=True)
    for t in range(32):
        place = t // 8 * 4 + t % 4
        which = pl.ds((t // 4 + idx[Y_HI]) % 2, 1)
        for h in range(2):
            lanes = slice((2 * t + h) * 128, (2 * t + h + 1) * 128)
            block = (w[:, lanes].astype(F32) * scale).astype(BF)
            out[place, which, 32 + 64 * h : 96 + 64 * h, :] = block[None]
    for g in range(8):
        keys = w[:, 8192 + g * 128 : 8320 + g * 128]
        values = w[:, 9216 + g * 128 : 9344 + g * 128]
        both = (jnp.concatenate([keys, values], 1).astype(F32) * scale).astype(BF)
        packed = dot(both[:32], sel[0]) + dot(both[32:], sel[1])
        which = pl.ds((g + idx[Y_HI]) % 2, 1)
        for i in range(4):
            block = packed[:, i * 128 : (i + 1) * 128].astype(BF)
            out[g // 2 * 4 + i, which, :32, :] = block[None]


def pack(idx, w_qkv, gain, sel):
    return call(
        pack_body,
        "pack_weights",
        [SM, VM, VM, VM],
        shape((16, 2, 160, 128)),
        VM,
        cost(0),
    )(idx, w_qkv, gain, sel)


def cut_body(src, kv, q):
    kv[...] = src[:, 1, :32, :]
    q[...] = src[:, 0, 32:, :]


def cut_first(src, after):
    return call(
        cut_body,
        "cut_first",
        [VM],
        [shape((16, 32, 128)), shape((16, 128, 128))],
        [VM] * 2,
        cost(0),
        after=after,
    )(src)


def cut_q_body(src, q):
    q[...] = src[:, 1, 32:, :]


def cut_second(src, after):
    return call(
        cut_q_body, "cut_second", [VM], shape((16, 128, 128)), VM, cost(0), after=after
    )(src)


def near_body(lo, hi, src, got, out):
    out[0] = src[:, 0, lo:hi, :]
    out[1] = got[...]


def near_rows(lo, hi, src, got, after, name):
    return call(
        functools.partial(near_body, lo, hi),
        name,
        [VM, VM],
        shape((2, 16, hi - lo, 128)),
        VM,
        cost(0),
        after=after,
    )(src, got)


def row_groups(idx, own, mate, side, far):
    p, s, y = idx[PAIR], idx[SIDE], idx[Y_HI]
    for ref, core, here in ((own, p, s), (mate, 1 - p, s), (side, p, 1 - s), (far, 1 - p, 1 - s)):
        yield ref, 0, 2 * core + here, y
        yield ref, 1, 2 * core + 1 - here, 1 - y


def norm_body(idx, x, out, residual, buf, sem):
    columns = pl.ds(pl.multiple_of(idx[TP] * 256, 256), 256)
    copies = [
        pltpu.make_async_copy(x.at[pl.ds(i * 128, 128)], buf.at[i % 4], sem.at[i])
        for i in range(8)
    ]
    for copy in copies[:4]:
        copy.start()
    for i in range(8):
        copies[i].wait()
        rows = slice(i * 128, (i + 1) * 128)
        square = jnp.zeros((128, 128), F32)
        for c in range(64):
            piece = buf[i % 4, :, c * 128 : (c + 1) * 128].astype(F32)
            square += piece * piece
        mean = jnp.sum(square, axis=1, keepdims=True) * (1.0 / D)
        out[rows, :] = jnp.broadcast_to(lax.rsqrt(mean + 1e-6), (128, 128))
        residual[rows, :] = buf[i % 4, :, columns]
        if i < 4:
            copies[i + 4].start()


def norms(idx, x, after):
    return call(
        norm_body,
        "token_norms",
        [SM, AN],
        [shape((1024, 128), F32), shape((1024, 256))],
        [VM] * 2,
        cost(0),
        [pltpu.VMEM((4, 128, D), BF), pltpu.SemaphoreType.DMA((8,))],
        after,
        50,
    )(idx, x)


def kv_sums(idx, x, groups, unpack, ws):
    acc = None
    for k, (ref, i, block, y) in enumerate(groups):
        both = dot(ref[i].reshape(512, 128), unpack[...]).astype(BF).reshape(4, 4, 32, 256)
        for z in range(4):
            ws[k, z, :, :32, :] = both[z, :, :, :128]
            ws[k, z, :, 32:, :] = both[z, :, :, 128:]
        for z in range(4):
            start = pl.multiple_of(block * 2048 + z * 512 + y * 256, 256)
            term = dot(x[:, pl.ds(start, 256)], ws[k, z].reshape(256, 128))
            acc = term if acc is None else acc + term
    return acc


def kv_early_body(idx, x, own, mate, unpack, out, ws):
    groups = list(row_groups(idx, own, mate, own, mate))[:4]
    out[...] = kv_sums(idx, x, groups, unpack, ws)


def kv_body(idx, x, early, side, far, norm, unpack, bias, bsel, cos, sin, kv, ws):
    groups = list(row_groups(idx, side, far, side, far))[4:]
    acc = early[...] + kv_sums(idx, x, groups, unpack, ws)
    g = idx[KV_HEAD]
    part = idx[X]
    base = jnp.concatenate([bias[pl.ds(64 + g, 1), :], bias[pl.ds(72 + g, 1), :]], 1)
    base = dot(jnp.broadcast_to(base, (8, 256)).astype(BF), bsel[part])[0:1]
    cosine = cos[part]
    sine = sin[part]
    acc = acc * norm[...] + base
    lane = lax.broadcasted_iota(jnp.int32, (SPAN, 128), 1)
    for i in range(2):
        a = acc[i * 256 : (i + 1) * 256]
        b = acc[512 + i * 256 : 512 + (i + 1) * 256]
        left = a * cosine + pltpu.roll(a, 64, 1) * sine
        right = pltpu.roll(b, 64, 1) * cosine + b * sine
        kv[i * 256 : (i + 1) * 256] = jnp.where(lane < 64, left, right).astype(BF)


KV_ROWS = pltpu.VMEM((4, 4, 4, 64, 128), BF)


def early_keys_values(idx, x, ws, tab, after):
    return call(
        kv_early_body,
        "keys_values_early",
        [SM] + [VM] * 4,
        shape((1024, 128), F32),
        VM,
        cost(0),
        [KV_ROWS],
        after,
    )(idx, x, *ws, tab["unpack"])


def keys_values(idx, x, ws, norm, tab, bias, after):
    return call(
        kv_body,
        "keys_values",
        [SM] + [VM] * 10,
        shape((512, 128)),
        VM,
        cost(0),
        [KV_ROWS],
        after,
    )(
        idx, x, *ws, norm, tab["unpack"], bias, tab["bias_sel"], tab["k_cos"], tab["k_sin"]
    )


def join_body(idx, p0, p1, p2, p3, gather, keys, values):
    for half in range(2):
        both = jnp.zeros((512, 256), F32)
        for k, piece in enumerate((p0, p1, p2, p3)):
            both += dot(piece[...], gather[(idx[X] + 4 - k) % 4, half])
        keys[half * 512 : (half + 1) * 512] = both[:, :128].astype(BF)
        values[half * 512 : (half + 1) * 512] = both[:, 128:].astype(BF)


def join_kv(idx, pieces, tab, after):
    return call(
        join_body,
        "join_keys_values",
        [SM] + [VM] * 5,
        [shape((1024, 128))] * 2,
        [VM] * 2,
        cost(0),
        after=after,
    )(idx, *pieces, tab["gather"])


def run_rows(ref, z):
    rows = [ref[4 * z : 4 * z + 4, 64 * h : 64 * h + 64, :].reshape(256, 128) for h in range(2)]
    return jnp.concatenate(rows, 1)


def half_block(x, ref, block, y):
    acc = None
    for z in range(4):
        start = pl.multiple_of(block * 2048 + z * 512 + y * 256, 256)
        term = dot(x[:, pl.ds(start, 256)], run_rows(ref, z))
        acc = term if acc is None else acc + term
    return acc


def early_body(idx, x, own, mate, both, mates, out, ws):
    p, s, y = idx[PAIR], idx[SIDE], idx[Y_HI]
    acc = half_block(x, own, 2 * p + s, y) + half_block(x, mate, 2 * (1 - p) + s, y)
    for k, rows in enumerate((both, mates)):
        for z in range(4):
            ws[k, z, y] = run_rows(rows.at[0], z)
            ws[k, z, 1 - y] = run_rows(rows.at[1], z)
        core = p if k == 0 else 1 - p
        start = pl.multiple_of((2 * core + 1 - s) * 2048, 2048)
        acc += dot(x[:, pl.ds(start, 2048)], ws[k].reshape(2048, 256))
    out[...] = acc


def early_heads(idx, x, ws, after):
    return call(
        early_body,
        "project_early",
        [SM] + [VM] * 5,
        shape((1024, 256), F32),
        VM,
        cost(0),
        [pltpu.VMEM((2, 4, 2, 256, 256), BF)],
        after,
    )(idx, x, *ws)


def heads_body(
    idx, x, early, last, last_far, norm, bias, cos, sin, keys, values, first, second, acc
):
    p, s, y = idx[PAIR], idx[SIDE], 1 - idx[Y_HI]
    acc[...] = early[...] + half_block(x, last, 2 * p + s, y)
    acc[...] += half_block(x, last_far.at[0], 2 * (1 - p) + s, y)
    row = lax.broadcasted_iota(jnp.int32, (SPAN, SPAN), 0)
    col = lax.broadcasted_iota(jnp.int32, (SPAN, SPAN), 1)
    ones = jnp.ones((SPAN, HD), BF)
    for seq in range(4):
        rows = slice(seq * SPAN, (seq + 1) * SPAN)
        with_ones = jnp.concatenate([values[rows], ones], 1)
        for h in range(2):
            query = acc[rows, h * 128 : (h + 1) * 128] * norm[rows, :]
            query += bias[pl.ds(2 * idx[TP] + h, 1), :]
            query = (query * cos[...] + pltpu.roll(query, 64, 1) * sin[...]).astype(BF)
            scores = lax.dot_general(
                query, keys[rows], (((1,), (1,)), ((), ())), preferred_element_type=F32
            ) * (HD**-0.5)
            scores = jnp.where(row >= col, scores, -1e30)
            expo = jnp.exp(scores - jnp.max(scores, axis=1, keepdims=True)).astype(BF)
            mixed = dot(expo, with_ones)
            done = (mixed[:, :HD] / mixed[:, HD:]).astype(BF)
            (first, second)[h][rows, :] = done


def heads(idx, x, ws, norm, tab, bias, keys, values, after):
    return call(
        heads_body,
        "query_heads",
        [SM] + [VM] * 10,
        [shape((1024, 128))] * 2,
        [VM] * 2,
        cost(0),
        [pltpu.VMEM((1024, 256), F32)],
        after,
    )(idx, x, *ws, norm, bias, tab["q_cos"], tab["q_sin"], keys, values)


def beside_body(idx, att, across, out):
    same = idx[Y_HI] == idx[PAIR]
    out[:, :128] = jnp.where(same, att[...], across[...])
    out[:, 128:] = jnp.where(same, across[...], att[...])


def beside(idx, att, across, after):
    return call(
        beside_body,
        "beside",
        [SM, VM, VM],
        shape((1024, 256)),
        VM,
        cost(0),
        after=after,
    )(idx, att, across)


def stack_body(*refs):
    for i, ref in enumerate(refs[:-1]):
        refs[-1][i] = ref[...]


def stack(name, arrays, after):
    dims = (len(arrays),) + arrays[0].shape
    return call(
        stack_body,
        name,
        [VM] * len(arrays),
        shape(dims),
        VM,
        cost(0),
        after=after,
    )(*arrays)


def pick_body(idx, here, across, keep, send):
    p = idx[PAIR]
    for i, w in enumerate((here, across)):
        side = idx[SIDE] if i == 0 else 1 - idx[SIDE]
        keep[side] = w[pl.ds(pl.multiple_of(p * 1024, 1024), 1024), :]
        send[side] = w[pl.ds(pl.multiple_of((1 - p) * 1024, 1024), 1024), :]


def pick(idx, here, across, after):
    return call(
        pick_body,
        "pick_rows",
        [SM, VM, VM],
        [shape((2, 1024, 256))] * 2,
        [VM] * 2,
        cost(0),
        after=after,
    )(idx, here, across)


def route_body(idx, keep, recv, stay, leave):
    for r, out in enumerate((stay.at[0], stay.at[1], leave.at[0], leave.at[1])):
        goal = idx[Z] ^ r
        same = goal // 2 == idx[PAIR]

        @pl.when(same)
        def _():
            out[...] = keep[goal % 2]

        @pl.when(jnp.logical_not(same))
        def _():
            out[...] = recv[goal % 2]


def route(idx, keep, recv, after):
    return call(
        route_body,
        "route_rows",
        [SM, VM, VM],
        [shape((2, 1024, 256))] * 2,
        [VM] * 2,
        cost(0),
        after=after,
    )(idx, keep, recv)


def second_body(stay, came, near, out):
    near[0] = stay[0]
    near[1] = came[0]
    out[0] = stay[1]
    out[1] = came[1]


def second_hop(stay, came, after):
    return call(
        second_body,
        "second_rows",
        [VM, VM],
        [shape((2, 1024, 256))] * 2,
        [VM] * 2,
        cost(0),
        after=after,
    )(stay, came)


def w_rows(w, other, i, part):
    rows = []
    for h in range(2):
        for ref in (w, other):
            rows.append(ref[i, pl.ds(pl.multiple_of(part * 256 + h * 128, 128), 128), :])
    return jnp.concatenate(rows, 0)


def out_body(r, idx, h0, h1, h2, h3, there, a0, a1, a2, a3, own, other, out):
    same = idx[Y_HI] == idx[PAIR]
    i = r // 2 if r % 2 == 0 else (idx[Z] + (r + 1) // 2) % 2
    acc = None
    for k, (here, both) in enumerate(zip((h0, h1, h2, h3), (a0, a1, a2, a3))):
        near = here[...]
        far = there[k]
        lanes = jnp.concatenate(
            [jnp.where(same, near, far), jnp.where(same, far, near), both[...]], 1
        )
        term = dot(lanes, w_rows(own, other, i, (idx[X] + 4 - k) % 4))
        acc = term if acc is None else acc + term
    out[...] = acc.astype(BF)


def project_out(r, idx, here, there, both, own, other, after):
    return call(
        functools.partial(out_body, r),
        f"project_out_{r}",
        [SM] + [VM] * 11,
        shape((1024, 256)),
        VM,
        cost(0),
        after=after,
    )(idx, *here, there, *both, own, other)


def finish_body(residual, p0, p1, p2, p3, out):
    total = residual[...].astype(F32)
    for part in (p0, p1, p2, p3):
        total += part[...].astype(F32)
    out[...] = total.astype(BF)


def finish(residual, parts):
    return call(
        finish_body, "add_residual", [VM] * 5, shape((1024, 256)), VM, cost(0)
    )(residual, *parts)


SWAP = [(0, 1), (1, 0)]


def shift(dz, dy, dx):
    return [
        (
            z * 8 + y * 4 + x,
            (z + dz) % 4 * 8 + (y + dy) % 2 * 4 + (x + dx) % 4,
        )
        for z in range(4)
        for y in range(2)
        for x in range(4)
    ]


def flip(bits):
    return [(t, t ^ bits) for t in range(32)]


PLANES = [[z * 8 + y * 4 + x for z in range(4) for x in range(4)] for y in range(2)]
DIAGONAL = [
    (s * 32 + t, (1 - s) * 32 + (t ^ 4)) for s in range(2) for t in range(32)
]


def shards(tokens, norm_gain, w_qkv, qkv_bias, w_out):
    tab = tables()
    seqs, span, width = tokens.shape
    p = lax.axis_index("pair")
    s = lax.axis_index("side")
    t = lax.axis_index("tp")
    idx = jnp.stack([t, t // 4, t % 4, p, t // 4 % 2, t // 8, s]).astype(jnp.int32)
    bias = qkv_bias.reshape(80, 128).astype(F32)
    x = tokens.reshape(seqs * span, width)

    w_across = lax.ppermute(w_out, "side", SWAP)
    packed = pack(idx, w_qkv, norm_gain.reshape(64, 128), tab["pack"])
    blocks = lax.all_to_all(
        packed, "tp", split_axis=0, concat_axis=0, tiled=True, axis_index_groups=PLANES
    )
    norm, residual = norms(idx, x, [packed])
    keep, send = pick(idx, w_out, w_across, [norm])
    kv_other, q_own = cut_first(blocks, [keep])
    q_side = lax.ppermute(q_own, "side", SWAP)
    kv_got = lax.ppermute(kv_other, ("side", "tp"), DIAGONAL)
    stay, leave = route(idx, keep, lax.ppermute(send, "pair", SWAP), [q_own])
    kv_own = near_rows(0, 32, blocks, kv_got, [stay], "near_kv")
    kv_side = lax.ppermute(kv_own, "side", SWAP)
    kv_mate = lax.ppermute(kv_own, "pair", SWAP)
    q_other = cut_second(blocks, [kv_own])
    q_got = lax.ppermute(q_other, ("side", "tp"), DIAGONAL)
    kv_early = early_keys_values(idx, x, (kv_own, kv_mate), tab, [q_other])
    kv_late = stack("late_kv", [kv_side], [kv_early])
    kv_far = lax.ppermute(kv_late, "pair", SWAP).reshape(kv_side.shape)
    q_mate = lax.ppermute(q_own, "pair", SWAP)
    q_both = stack("late_queries", [q_side, q_got], [kv_late])
    q_mates = lax.ppermute(q_both, "pair", SWAP)
    kv_piece = keys_values(
        idx, x, (kv_early, kv_side, kv_far), norm, tab, bias, [q_mate, q_mates]
    )
    got_side = lax.ppermute(q_got, "side", SWAP)
    pieces = [kv_piece] + [
        lax.ppermute(kv_piece, "tp", shift(0, 0, r)) for r in range(1, 4)
    ]
    came = lax.ppermute(leave, "tp", flip(16))
    early = early_heads(
        idx,
        x,
        (q_own, q_mate, q_both, q_mates),
        [kv_piece],
    )
    late = stack("late_q", [got_side], [early, pieces[1], pieces[3]])
    keys, values = join_kv(idx, pieces, tab, [late])
    late_far = lax.ppermute(late, "pair", SWAP)
    ws = (early, got_side, late_far)
    att0, att1 = heads(idx, x, ws, norm, tab, bias, keys, values, [])
    near, hop = second_hop(stay, came, [att0])
    near_other = lax.ppermute(near, "pair", SWAP)
    last = lax.ppermute(hop, "tp", flip(8))
    last_other = lax.ppermute(last, "pair", SWAP)
    here = [att0] + [lax.ppermute(att0, "tp", shift(0, 0, r)) for r in range(1, 4)]
    stacked = stack("stack_head0", here, [near])
    there = lax.ppermute(stacked, "tp", shift(0, 1, 0))
    both = beside(idx, att1, lax.ppermute(att1, "tp", shift(0, 1, 0)), [stacked, near_other])
    plane = [both] + [lax.ppermute(both, "tp", shift(0, 0, r)) for r in range(1, 4)]

    parts = []
    for r in (2, 1, 3, 0):
        w, w_other = (last, last_other) if r % 2 else (near, near_other)
        parts.append(
            project_out(r, idx, here, there, plane, w, w_other, [both, *parts[-1:]])
        )
    parts = [
        lax.ppermute(part, "tp", shift(-r, 0, 0)) if r else part
        for r, part in zip((2, 1, 3, 0), parts)
    ]
    return finish(residual, parts).reshape(seqs, span, 256)


def solution(mesh):
    placed = (
        P(("pair", "side"), None, None),
        P(),
        P(("pair", "side", "tp"), None),
        P(),
        P(("pair", "side"), "tp"),
    )
    return jax.shard_map(
        shards,
        mesh=mesh,
        in_specs=placed,
        out_specs=P(("pair", "side"), None, "tp"),
        check_vma=False,
    )
```
